32 devices in a mesh: mode: 2 (over x), space: 16 (over z, y, core).
Axes of the slice: x: 2, y: 2, z: 4, core: 2. Of those that a mesh axis runs over, the one named last changes fastest.
Arguments:
- mode_fields: bfloat16 [128, 2, 64, 256], P('mode', None, 'space'), may hold values from -6 to 6
- metric: float32 [3, 64, 256], P(None, 'space'), may hold values from 0.5 to 2
- plan: int32 [4, 2], replicated, may hold values from 0 to 1, as said below
Outputs:
- tensor: float32 [4096, 128], P('space', 'mode')
The draws below stay inside these ranges and needn't reach their ends.
Inputs may be any that keep to these rules, and one draw needn't show every extreme that they name: `plan`: rows 0 and 1 name the advecting blocks, rows 2 and 3 the advected blocks: column 0 a mode group, column 1 a half of its modes (0 or 1). Blocks may repeat.
All inputs are finite; a program needn't handle non-finite values.
Results may differ from the reference program's by a relative error of at most 0.0041.
Values may be sent and summed in bfloat16 or wider, within the bound.
A program may use at most 64 MiB of HBM per device.

```python
import math
import jax
import jax.numpy as jnp
from jax import lax

MODE_DEV = 64
MODES = 128
BLOCK = 32
NY = 256
NX = 64
N_MODE = 2


def draw_plan(key, part):
    first_key, second_key, third_key, fourth_key = jax.random.split(jax.random.fold_in(key, 17), 4)
    owners = jax.random.randint(first_key, (4,), 0, N_MODE)
    halves = jax.random.randint(second_key, (4,), 0, 2)
    top_slot = jax.random.randint(third_key, (), 0, 4)
    low_slot = jax.random.randint(fourth_key, (), 0, 4)
    places = jnp.arange(4)
    owners = jnp.where(places == top_slot, N_MODE - 1, owners)
    halves = jnp.where(places == low_slot, 0, halves)
    return jnp.stack([owners, halves], axis=1).astype(jnp.int32)


def block_scale(rng, shape, pieces, least, largest):
    gain = 1.0
    for position, blocks in pieces:
        steps = jax.random.uniform(jax.random.fold_in(jax.random.fold_in(rng, 6), position), (blocks,), jnp.float32, least / len(pieces), largest / len(pieces))
        gain = gain * jnp.repeat(jnp.exp(steps), shape[position] // blocks).reshape((-1,) + (1,) * (len(shape) - 1 - position))
    return gain


def scatter_about(key, shape, deviation, most, cuts=(), kind=jnp.bfloat16):
    array = jax.random.normal(key, shape, jnp.float32) * deviation
    if len(cuts) > 0:
        array = block_scale(key, shape, cuts, -0.22, 0.18) * array
    return jnp.clip(array, min=-most, max=most).astype(kind)


def setup_inputs(seed: int = 0) -> dict:
    splits = jax.random.split(jax.random.key(seed), 4)
    mode_fields = scatter_about(splits[0], (MODES, 2, NX, NY), 1.0, 6.0, ((0, 2), (2, 16)))
    metric = jnp.clip(jnp.exp(math.log(2.0) - 1.3862944 * jax.random.uniform(splits[1], (3, NX, NY), jnp.float32) ** block_scale(splits[1], (3, NX, NY), ((1, 16),), -0.2, 0.2)), 0.5, 2.0)
    plan = draw_plan(jax.random.fold_in(splits[3], 71), 0)
    return {"mode_fields": mode_fields, "metric": metric, "plan": plan}


def stencil(padded, metric):
    widened = padded.astype(jnp.float32)
    along_x = (widened[:, :, 2:, :] - widened[:, :, :-2, :]) * metric[0]
    interior = jnp.pad(widened[:, :, 1:-1, :], ((0, 0), (0, 0), (0, 0), (1, 1)))
    along_y = (interior[:, :, :, 2:] - interior[:, :, :, :-2]) * metric[1]
    return jnp.stack((along_x, along_y), axis=1).astype(jnp.bfloat16)


def advect(column, slopes, weight):
    widened = column.astype(jnp.float32)
    mixed = widened[0] * slopes[:, 0].astype(jnp.float32) + widened[1] * slopes[:, 1].astype(jnp.float32)
    return (mixed * weight).astype(jnp.bfloat16).reshape(slopes.shape[0], -1)


def reference(mode_fields, metric, plan):
    def own_block(source_row):
        first_row = plan[source_row, 0] * MODE_DEV + plan[source_row, 1] * BLOCK
        return lax.dynamic_slice_in_dim(mode_fields, first_row.astype(jnp.int32), BLOCK, 0)

    movers = jnp.concatenate([own_block(0), own_block(1)], axis=0)
    carried = jnp.concatenate([own_block(2), own_block(3)], axis=0)
    padded = jnp.pad(carried, ((0, 0), (0, 0), (1, 1), (0, 0)))
    slopes = stencil(padded, metric)
    test_rows = mode_fields.reshape(MODES, -1)

    def project(column):
        advected_field = advect(column, slopes, metric[2])
        return lax.dot_general(advected_field, test_rows, (((1,), (1,)), ((), ())), preferred_element_type=jnp.float32)

    blocks = lax.map(project, movers)
    return blocks.reshape(-1, MODES) * (float(NX * NY) ** -0.5)
```

```python
import functools

import jax
import jax.numpy as jnp
from jax import lax
from jax.experimental import pallas as pl
from jax.experimental.pallas import tpu as pltpu
from jax.sharding import PartitionSpec as P

MESH = pl.DeviceIdType.MESH
F32 = jnp.float32
BF16 = jnp.bfloat16


def kernel(
    n_mode, n, norm_factor,
    x_ref, metric_ref, plan_ref, out_ref,
    fields, slopes, movers, keep, send1, recv1, send2, recv2, send3, recv3,
    x_send, x_recv, h_send, h_recv, s1_send, s1_recv, s2_send, s2_recv, s3_send, s3_recv,
):
    R, _, half, width = x_ref.shape
    modes = 2 * half
    L = metric_ref.shape[2]
    C = width // L
    nq, nz = n // 2, n // 4
    jb = movers.shape[3]

    me = lax.axis_index("mode")
    s = lax.axis_index("space")
    core = lax.rem(s, 2)
    pair = s // 2
    y = lax.rem(pair, 2)
    z = pair // 2
    twin = s + 1 - 2 * core
    across = s + 2 - 4 * y
    has_left = s > 0
    has_right = s < n - 1
    has_other = ((core == 1) & has_right) | ((core == 0) & has_left)
    other = jnp.clip(s + 2 * core - 1, 0, n - 1)

    def along(step):
        return (lax.rem(z + step, nz) * 2 + y) * 2 + core

    barrier = pltpu.get_barrier_semaphore()

    def greet(device):
        pl.semaphore_signal(barrier, inc=1, device_id=device, device_id_type=MESH)

    for d in range(1, n_mode):
        greet((lax.rem(me + d, n_mode), s))
    greet((me, twin))
    greet((me, across))
    for step in range(1, nz):
        greet((me, along(step)))

    @pl.when(has_other)
    def _():
        greet((me, other))

    greeted = (n_mode - 1) + 2 + (nz - 1)
    pl.semaphore_wait(barrier, jnp.where(has_other, greeted + 1, greeted))

    def remote(src, dst, send, recv, device):
        return pltpu.make_async_remote_copy(
            src_ref=src, dst_ref=dst, send_sem=send, recv_sem=recv,
            device_id=device, device_id_type=MESH,
        )

    def spread(d, piece):
        peer = (lax.rem(me + d, n_mode), s)
        rows = ((0, 1), (R - 1, 1), (1, R - 2))[piece]
        return remote(
            x_ref.at[pl.ds(rows[0], rows[1])],
            fields.at[me, pl.ds(1 + rows[0], rows[1])],
            x_send.at[d, piece], x_recv.at[d, piece], peer,
        )

    def halo(d, side):
        group = lax.rem(me + n_mode - d, n_mode)
        if d == 0:
            src = x_ref.at[0 if side == 0 else R - 1]
        else:
            src = fields.at[group, 1 if side == 0 else R]
        target = (me, jnp.maximum(s - 1, 0)) if side == 0 else (me, jnp.minimum(s + 1, n - 1))
        return remote(
            src, fields.at[group, R + 1 if side == 0 else 0],
            h_send.at[d, side], h_recv.at[d, side], target,
        )

    for piece in range(3):
        for d in range(1, n_mode):
            spread(d, piece).start()

    def start_halo(d):
        @pl.when(has_left)
        def _():
            halo(d, 0).start()

        @pl.when(has_right)
        def _():
            halo(d, 1).start()

    start_halo(0)
    for r in range(R):
        fields[me, 1 + r] = x_ref[r]

    @pl.when(jnp.logical_not(has_left))
    def _():
        for g in range(n_mode):
            fields[g, 0] = jnp.zeros_like(fields[g, 0])

    @pl.when(jnp.logical_not(has_right))
    def _():
        for g in range(n_mode):
            fields[g, R + 1] = jnp.zeros_like(fields[g, R + 1])

    for d in range(1, n_mode):
        spread(d, 0).wait_recv()
        spread(d, 1).wait_recv()
        start_halo(d)
    for d in range(1, n_mode):
        spread(d, 2).wait_recv()
    for d in range(n_mode):
        @pl.when(has_right)
        def _():
            halo(d, 0).wait_recv()

        @pl.when(has_left)
        def _():
            halo(d, 1).wait_recv()

    lane = lax.rem(lax.broadcasted_iota(jnp.int32, (half, width), 1), L)
    for b in range(2):
        owner, which = plan_ref[b, 0], plan_ref[b, 1]
        for r in range(R):
            block = fields[owner, 1 + r, which].astype(F32)
            weight = metric_ref[2, r : r + 1, :]
            for c in range(2):
                scaled = block[:, c * L : (c + 1) * L] * weight
                movers[c, r, pl.ds(b * (half // jb), half // jb)] = scaled.reshape(
                    half // jb, jb, L
                )
    for b in range(2):
        owner, which = plan_ref[2 + b, 0], plan_ref[2 + b, 1]
        for r in range(R):
            low = fields[owner, r, which].astype(F32)
            mid = fields[owner, r + 1, which].astype(F32)
            high = fields[owner, r + 2, which].astype(F32)
            first = jnp.concatenate([metric_ref[0, r : r + 1, :]] * C, axis=1)
            second = jnp.concatenate([metric_ref[1, r : r + 1, :]] * C, axis=1)
            after = jnp.where(lane == L - 1, 0.0, pltpu.roll(mid, width - 1, 1))
            before = jnp.where(lane == 0, 0.0, pltpu.roll(mid, 1, 1))
            place = slice(b * half, (b + 1) * half)
            slopes[0, r, place, :] = ((high - low) * first).astype(BF16).astype(F32)
            slopes[1, r, place, :] = ((after - before) * second).astype(BF16).astype(F32)

    def project(q):
        total = None
        for r in range(R):
            rows = []
            for j in range(jb):
                m0 = movers[0, r, q, j : j + 1, :]
                m1 = movers[1, r, q, j : j + 1, :]
                parts = []
                for c in range(C):
                    lanes = slice(c * L, (c + 1) * L)
                    mixed = m0 * slopes[0, r, :, lanes] + m1 * slopes[1, r, :, lanes]
                    parts.append(mixed.astype(BF16))
                rows.append(jnp.concatenate(parts, axis=1))
            part = lax.dot_general(
                jnp.concatenate(rows, axis=0), x_ref[r].reshape(modes, width),
                (((1,), (1,)), ((), ())), preferred_element_type=F32,
            )
            total = part if total is None else total + part
        return total

    def pack(rows):
        h = rows.shape[0] // 2
        return jnp.concatenate([rows[:h], rows[h:]], axis=1)

    def to_twin(it):
        return remote(
            send1.at[it], recv1.at[it], s1_send.at[it], s1_recv.at[it], (me, twin)
        )

    def to_across(t):
        return remote(
            send2.at[t], recv2.at[t], s2_send.at[t], s2_recv.at[t], (me, across)
        )

    def to_along(t):
        return remote(
            send3.at[t], recv3.at[t], s3_send.at[t], s3_recv.at[t], (me, along(t + 1))
        )

    def gathered(it):
        to_twin(it).wait_recv()
        return keep[it] + recv1[it].astype(F32)

    def step(it, carry):
        t = lax.rem(it, nz)
        column = jnp.where(it < nz, 1 - y, y)
        q = lax.rem(z + 1 + t, nz) * 2 + column
        total = project(q)
        rows = total.shape[0] // 2
        low, high = pack(total[:rows]), pack(total[rows:])
        keep[it] = jnp.where(core == 0, low, high)
        send1[it] = jnp.where(core == 0, high, low).astype(BF16)
        to_twin(it).start()

        @pl.when((it >= 1) & (it <= nz))
        def _():
            t = it - 1
            send2[t] = gathered(it - 1).astype(BF16)
            to_across(t).start()

        @pl.when(it > nz)
        def _():
            t = it - 1 - nz
            value = gathered(it - 1)
            to_across(t).wait_recv()
            send3[t] = (value + recv2[t].astype(F32)).astype(BF16)
            to_along(t).start()

        return carry

    lax.fori_loop(0, nq, step, 0)

    value = gathered(nq - 1)
    to_across(nz - 1).wait_recv()
    value = value + recv2[nz - 1].astype(F32)
    for t in range(nz - 1):
        to_along(t).wait_recv()
        value = value + recv3[t].astype(F32)
    value = value * norm_factor
    h = value.shape[0]
    out_ref[pl.ds(0, h), :] = value[:, :modes]
    out_ref[pl.ds(h, h), :] = value[:, modes:]

    for d in range(1, n_mode):
        for piece in range(3):
            spread(d, piece).wait_send()
    for d in range(n_mode):
        @pl.when(has_left)
        def _():
            halo(d, 0).wait_send()

        @pl.when(has_right)
        def _():
            halo(d, 1).wait_send()
    for it in range(nq):
        to_twin(it).wait_send()
    for t in range(nz):
        to_across(t).wait_send()
    for t in range(nz - 1):
        to_along(t).wait_send()


def body(mode_fields, metric, plan):
    n_mode, n = lax.axis_size("mode"), lax.axis_size("space")
    modes, C, R, L = mode_fields.shape
    half, width = modes // 2, C * L
    norm_factor = float(R * n * L) ** (-0.5)
    out_rows = modes * modes // n
    h = out_rows // 2
    nq, nz = n // 2, n // 4
    jb = modes // nq
    x = mode_fields.transpose(2, 0, 1, 3).reshape(R, 2, half, width)
    dma = pltpu.SemaphoreType.DMA
    return pl.pallas_call(
        functools.partial(kernel, n_mode, n, norm_factor),
        out_shape=jax.ShapeDtypeStruct((out_rows, modes), F32),
        in_specs=[
            pl.BlockSpec(memory_space=pltpu.VMEM),
            pl.BlockSpec(memory_space=pltpu.VMEM),
            pl.BlockSpec(memory_space=pltpu.SMEM),
        ],
        out_specs=pl.BlockSpec(memory_space=pltpu.VMEM),
        scratch_shapes=[
            pltpu.VMEM((n_mode, R + 2, 2, half, width), BF16),
            pltpu.VMEM((2, R, modes, width), F32),
            pltpu.VMEM((2, R, nq, jb, L), F32),
            pltpu.VMEM((nq, h, 2 * modes), F32),
            pltpu.VMEM((nq, h, 2 * modes), BF16),
            pltpu.VMEM((nq, h, 2 * modes), BF16),
            pltpu.VMEM((nz, h, 2 * modes), BF16),
            pltpu.VMEM((nz, h, 2 * modes), BF16),
            pltpu.VMEM((nz, h, 2 * modes), BF16),
            pltpu.VMEM((nz, h, 2 * modes), BF16),
            dma((n_mode, 3)),
            dma((n_mode, 3)),
            dma((n_mode, 2)),
            dma((n_mode, 2)),
            dma((nq,)),
            dma((nq,)),
            dma((nz,)),
            dma((nz,)),
            dma((nz,)),
            dma((nz,)),
        ],
        compiler_params=pltpu.CompilerParams(
            collective_id=0, has_side_effects=True, vmem_limit_bytes=40 * 1024 * 1024
        ),
    )(x, metric, plan)


def solution(mesh):
    return jax.shard_map(
        body,
        mesh=mesh,
        in_specs=(P("mode", None, "space", None), P(None, "space", None), P()),
        out_specs=P("space", "mode"),
        check_vma=False,
    )
```

```python
import functools

import jax
import jax.numpy as jnp
from jax import lax
from jax.experimental import pallas as pl
from jax.experimental.pallas import tpu as pltpu
from jax.sharding import PartitionSpec as P

MESH = pl.DeviceIdType.MESH
F32 = jnp.float32
BF16 = jnp.bfloat16


def kernel(
    n_mode, n, parts, norm_factor,
    x_ref, metric_ref, plan_ref, out_ref,
    fields, weights, slopes, movers, keep, send1, recv1, send2, recv2, send3, recv3,
    x_send, x_recv, h_send, h_recv, s1_send, s1_recv, s2_send, s2_recv, s3_send, s3_recv,
):
    R, _, half, width = x_ref.shape
    modes = 2 * half
    own = modes // parts
    L = metric_ref.shape[2]
    C = width // L
    nq, nz = n // 2, n // 4
    jb = movers.shape[3]

    me = lax.axis_index("mode")
    s = lax.axis_index("space")
    core = lax.rem(s, 2)
    pair = s // 2
    y = lax.rem(pair, 2)
    z = pair // 2
    twin = s + 1 - 2 * core
    across = s + 2 - 4 * y
    has_left = s > 0
    has_right = s < n - 1
    has_other = ((core == 1) & has_right) | ((core == 0) & has_left)
    other = jnp.clip(s + 2 * core - 1, 0, n - 1)

    def along(step):
        return (lax.rem(z + step, nz) * 2 + y) * 2 + core

    barrier = pltpu.get_barrier_semaphore()

    def greet(device):
        pl.semaphore_signal(barrier, inc=1, device_id=device, device_id_type=MESH)

    for d in range(1, n_mode):
        greet((lax.rem(me + d, n_mode), s))
    greet((me, twin))
    greet((me, across))
    for step in range(1, nz):
        for e in range(parts):
            greet((lax.rem(me + e, n_mode), along(step)))

    @pl.when(has_other)
    def _():
        greet((me, other))

    greeted = (n_mode - 1) + 2 + parts * (nz - 1)
    pl.semaphore_wait(barrier, jnp.where(has_other, greeted + 1, greeted))

    def remote(src, dst, send, recv, device):
        return pltpu.make_async_remote_copy(
            src_ref=src, dst_ref=dst, send_sem=send, recv_sem=recv,
            device_id=device, device_id_type=MESH,
        )

    def spread(d, piece):
        peer = (lax.rem(me + d, n_mode), s)
        rows = ((0, 1), (R - 1, 1), (1, R - 2))[piece]
        return remote(
            x_ref.at[pl.ds(rows[0], rows[1])],
            fields.at[me, pl.ds(1 + rows[0], rows[1])],
            x_send.at[d, piece], x_recv.at[d, piece], peer,
        )

    def halo(d, side):
        group = lax.rem(me + n_mode - d, n_mode)
        if d == 0:
            src = x_ref.at[0 if side == 0 else R - 1]
        else:
            src = fields.at[group, 1 if side == 0 else R]
        target = (me, jnp.maximum(s - 1, 0)) if side == 0 else (me, jnp.minimum(s + 1, n - 1))
        return remote(
            src, fields.at[group, R + 1 if side == 0 else 0],
            h_send.at[d, side], h_recv.at[d, side], target,
        )

    for piece in range(3):
        for d in range(1, n_mode):
            spread(d, piece).start()

    def start_halo(d):
        @pl.when(has_left)
        def _():
            halo(d, 0).start()

        @pl.when(has_right)
        def _():
            halo(d, 1).start()

    start_halo(0)
    for r in range(R):
        fields[me, 1 + r] = x_ref[r]

    @pl.when(jnp.logical_not(has_left))
    def _():
        for g in range(n_mode):
            fields[g, 0] = jnp.zeros_like(fields[g, 0])

    @pl.when(jnp.logical_not(has_right))
    def _():
        for g in range(n_mode):
            fields[g, R + 1] = jnp.zeros_like(fields[g, R + 1])

    for d in range(1, n_mode):
        spread(d, 0).wait_recv()
        spread(d, 1).wait_recv()
        start_halo(d)
    for d in range(1, n_mode):
        spread(d, 2).wait_recv()
    for d in range(n_mode):
        @pl.when(has_right)
        def _():
            halo(d, 0).wait_recv()

        @pl.when(has_left)
        def _():
            halo(d, 1).wait_recv()

    lane = lax.rem(lax.broadcasted_iota(jnp.int32, (half, width), 1), L)
    for b in range(2):
        owner, which = plan_ref[0, b], plan_ref[1, b]
        for r in range(R):
            block = fields[owner, 1 + r, which].astype(F32)
            weight = metric_ref[2, r : r + 1, :]
            for c in range(2):
                scaled = block[:, c * L : (c + 1) * L] * weight
                movers[c, r, pl.ds(b * (half // jb), half // jb)] = scaled.reshape(
                    half // jb, jb, L
                )
    for b in range(2 // parts):
        source = 2 + b if parts == 1 else 2 + me
        owner, which = plan_ref[0, source], plan_ref[1, source]
        for r in range(R):
            low = fields[owner, r, which].astype(F32)
            mid = fields[owner, r + 1, which].astype(F32)
            high = fields[owner, r + 2, which].astype(F32)
            first = jnp.concatenate([metric_ref[0, r : r + 1, :]] * C, axis=1)
            second = jnp.concatenate([metric_ref[1, r : r + 1, :]] * C, axis=1)
            after = jnp.where(lane == L - 1, 0.0, pltpu.roll(mid, width - 1, 1))
            before = jnp.where(lane == 0, 0.0, pltpu.roll(mid, 1, 1))
            place = slice(b * half, (b + 1) * half)
            slopes[0, r, place, :] = ((high - low) * first).astype(BF16).astype(F32)
            slopes[1, r, place, :] = ((after - before) * second).astype(BF16).astype(F32)
    for r in range(R):
        if parts == 1:
            tests = x_ref[r].reshape(modes, width)
        else:
            tests = jnp.concatenate(
                [fields[g, 1 + r].reshape(modes, width) for g in range(n_mode)], axis=0
            )
        weights[r] = tests.T

    tile = 16

    def project(q):
        total = None
        for r in range(R):
            m = [
                [jnp.broadcast_to(movers[d, r, q, j : j + 1, :], (tile, L)) for j in range(jb)]
                for d in range(2)
            ]
            rows = []
            for k in range(0, own, tile):
                parted = [[] for _ in range(jb)]
                for c in range(C):
                    lanes = slice(c * L, (c + 1) * L)
                    s0 = slopes[0, r, k : k + tile, lanes]
                    s1 = slopes[1, r, k : k + tile, lanes]
                    for j in range(jb):
                        parted[j].append((m[0][j] * s0 + m[1][j] * s1).astype(BF16))
                rows += [jnp.concatenate(parted[j], axis=1) for j in range(jb)]
            part = jnp.dot(
                jnp.concatenate(rows, axis=0), weights[r], preferred_element_type=F32
            )
            total = part if total is None else total + part
        order = [total[(k * jb + j) * tile : (k * jb + j + 1) * tile]
                 for j in range(jb) for k in range(own // tile)]
        return jnp.concatenate(order, axis=0)

    def pack(rows):
        h = rows.shape[0] // 2
        return jnp.concatenate([rows[:h], rows[h:]], axis=1)

    def to_twin(it):
        return remote(
            send1.at[it], recv1.at[it], s1_send.at[it], s1_recv.at[it], (me, twin)
        )

    def to_across(t):
        return remote(
            send2.at[t], recv2.at[t], s2_send.at[t], s2_recv.at[t], (me, across)
        )

    def to_along(t, e):
        return remote(
            send3.at[t, e], recv3.at[t, e], s3_send.at[t, e], s3_recv.at[t, e],
            (lax.rem(me + e, n_mode), along(t + 1)),
        )

    def columns(value):
        if parts == 1:
            return [value]
        low, high = pack(value[:, :modes]), pack(value[:, modes:])
        return [jnp.where(me == 0, low, high), jnp.where(me == 0, high, low)]

    def gathered(it):
        to_twin(it).wait_recv()
        return keep[it] + recv1[it].astype(F32)

    def step(it, carry):
        t = lax.rem(it, nz)
        column = jnp.where(it < nz, 1 - y, y)
        q = lax.rem(z + 1 + t, nz) * 2 + column
        total = project(q)
        rows = total.shape[0] // 2
        low, high = total[:rows], total[rows:]
        if parts == 1:
            low, high = pack(low), pack(high)
        keep[it] = jnp.where(core == 0, low, high)
        send1[it] = jnp.where(core == 0, high, low).astype(BF16)
        to_twin(it).start()

        @pl.when((it >= 1) & (it <= nz))
        def _():
            t = it - 1
            send2[t] = gathered(it - 1).astype(BF16)
            to_across(t).start()

        @pl.when(it > nz)
        def _():
            t = it - 1 - nz
            value = gathered(it - 1)
            to_across(t).wait_recv()
            for e, piece in enumerate(columns(value + recv2[t].astype(F32))):
                send3[t, e] = piece.astype(BF16)
                to_along(t, e).start()

        return carry

    lax.fori_loop(0, nq, step, 0)

    value = gathered(nq - 1)
    to_across(nz - 1).wait_recv()
    pieces = columns(value + recv2[nz - 1].astype(F32))
    if parts == 2:
        send3[nz - 1, 1] = pieces[1].astype(BF16)
        to_along(nz - 1, 1).start()
    for e in range(parts):
        value = pieces[0] if e == 0 else None
        for t in range(nz if e else nz - 1):
            to_along(t, e).wait_recv()
            got = recv3[t, e].astype(F32)
            value = got if value is None else value + got
        value = value * norm_factor
        halves = [value[:, :modes], value[:, modes:]]
        if parts == 1:
            h = value.shape[0]
            out_ref[pl.ds(0, h), :] = halves[0]
            out_ref[pl.ds(h, h), :] = halves[1]
        else:
            value = jnp.concatenate(halves, axis=0)
            column = me if e == 0 else 1 - me
            for j in range(value.shape[0] // own):
                start = pl.multiple_of(j * modes + column * own, own)
                out_ref[pl.ds(start, own), :] = value[j * own : (j + 1) * own]

    for d in range(1, n_mode):
        for piece in range(3):
            spread(d, piece).wait_send()
    for d in range(n_mode):
        @pl.when(has_left)
        def _():
            halo(d, 0).wait_send()

        @pl.when(has_right)
        def _():
            halo(d, 1).wait_send()
    for it in range(nq):
        to_twin(it).wait_send()
    for t in range(nz):
        to_across(t).wait_send()
    for t in range(nz):
        for e in range(parts):
            if t < nz - 1 or e > 0:
                to_along(t, e).wait_send()


def body(mode_fields, metric, plan):
    n_mode, n = lax.axis_size("mode"), lax.axis_size("space")
    modes, C, R, L = mode_fields.shape
    half, width = modes // 2, C * L
    norm_factor = float(R * n * L) ** (-0.5)
    out_rows = modes * modes // n
    h = out_rows // 2
    nq, nz = n // 2, n // 4
    jb = modes // nq
    parts = 2 if n_mode == 2 else 1
    x = mode_fields.transpose(2, 0, 1, 3).reshape(R, 2, half, width)
    dma = pltpu.SemaphoreType.DMA
    return pl.pallas_call(
        functools.partial(kernel, n_mode, n, parts, norm_factor),
        out_shape=jax.ShapeDtypeStruct((out_rows, modes), F32),
        in_specs=[
            pl.BlockSpec(memory_space=pltpu.VMEM),
            pl.BlockSpec(memory_space=pltpu.VMEM),
            pl.BlockSpec(memory_space=pltpu.SMEM),
        ],
        out_specs=pl.BlockSpec(memory_space=pltpu.VMEM),
        scratch_shapes=[
            pltpu.VMEM((n_mode, R + 2, 2, half, width), BF16),
            pltpu.VMEM((R, width, modes * parts), BF16),
            pltpu.VMEM((2, R, modes // parts, width), F32),
            pltpu.VMEM((2, R, nq, jb, L), F32),
            pltpu.VMEM((nq, h, 2 * modes), F32),
            pltpu.VMEM((nq, h, 2 * modes), BF16),
            pltpu.VMEM((nq, h, 2 * modes), BF16),
            pltpu.VMEM((nz, h, 2 * modes), BF16),
            pltpu.VMEM((nz, h, 2 * modes), BF16),
            pltpu.VMEM((nz, parts, h // parts, 2 * modes), BF16),
            pltpu.VMEM((nz, parts, h // parts, 2 * modes), BF16),
            dma((n_mode, 3)),
            dma((n_mode, 3)),
            dma((n_mode, 2)),
            dma((n_mode, 2)),
            dma((nq,)),
            dma((nq,)),
            dma((nz,)),
            dma((nz,)),
            dma((nz, parts)),
            dma((nz, parts)),
        ],
        compiler_params=pltpu.CompilerParams(
            collective_id=0, has_side_effects=True, vmem_limit_bytes=40 * 1024 * 1024
        ),
    )(x, metric, plan.T)


def solution(mesh):
    return jax.shard_map(
        body,
        mesh=mesh,
        in_specs=(P("mode", None, "space", None), P(None, "space", None), P()),
        out_specs=P("space", "mode"),
        check_vma=False,
    )
```

```python
import functools

import jax
import jax.numpy as jnp
from jax import lax
from jax.experimental import pallas as pl
from jax.experimental.pallas import tpu as pltpu
from jax.sharding import PartitionSpec as P

MESH = pl.DeviceIdType.MESH
F32 = jnp.float32
BF16 = jnp.bfloat16


def kernel(
    n_mode, n, parts, norm_factor,
    x_ref, metric_hbm, plan_hbm, out_ref,
    metric_ref, plan_ref, result, partial, weights, slopes, movers, keep, send1, recv1, send2, recv2, send3, recv3,
    load_sem, x_send, x_recv, h_send, h_recv, s1_send, s1_recv, s2_send, s2_recv, s3_send, s3_recv, *fields,
):
    R, _, half, width = x_ref.shape
    modes = 2 * half
    own = modes // parts
    L = metric_ref.shape[2]
    C = width // L
    nq, nz = n // 2, n // 4
    jb = movers.shape[3]

    me = lax.axis_index("mode")
    s = lax.axis_index("space")
    core = lax.rem(s, 2)
    pair = s // 2
    y = lax.rem(pair, 2)
    z = pair // 2
    twin = s + 1 - 2 * core
    across = s + 2 - 4 * y
    has_left = s > 0
    has_right = s < n - 1
    has_other = ((core == 1) & has_right) | ((core == 0) & has_left)
    other = jnp.clip(s + 2 * core - 1, 0, n - 1)

    def along(step):
        return (lax.rem(z + step, nz) * 2 + y) * 2 + core

    load_metric = pltpu.make_async_copy(metric_hbm, metric_ref, load_sem.at[0])
    load_plan = pltpu.make_async_copy(plan_hbm, plan_ref, load_sem.at[1])
    load_metric.start()
    load_plan.start()

    barrier = pltpu.get_barrier_semaphore()

    def greet(device):
        pl.semaphore_signal(barrier, inc=1, device_id=device, device_id_type=MESH)

    for d in range(1, n_mode):
        greet((lax.rem(me + d, n_mode), s))
    greet((me, twin))
    greet((me, across))
    for step in range(1, nz):
        for e in range(parts):
            greet((lax.rem(me + e, n_mode), along(step)))

    @pl.when(has_other)
    def _():
        greet((me, other))

    greeted = (n_mode - 1) + 2 + parts * (nz - 1)
    pl.semaphore_wait(barrier, jnp.where(has_other, greeted + 1, greeted))

    def remote(src, dst, send, recv, device):
        return pltpu.make_async_remote_copy(
            src_ref=src, dst_ref=dst, send_sem=send, recv_sem=recv,
            device_id=device, device_id_type=MESH,
        )

    def spread(d, row):
        return remote(
            x_ref.at[row], fields[1 + row].at[me],
            x_send.at[d, row], x_recv.at[d, row], (lax.rem(me + d, n_mode), s),
        )

    def halo(d, side):
        group = lax.rem(me + n_mode - d, n_mode)
        if d == 0:
            src = x_ref.at[0 if side == 0 else R - 1]
        else:
            src = fields[1 if side == 0 else R].at[group]
        target = (me, jnp.maximum(s - 1, 0)) if side == 0 else (me, jnp.minimum(s + 1, n - 1))
        return remote(
            src, fields[R + 1 if side == 0 else 0].at[group],
            h_send.at[d, side], h_recv.at[d, side], target,
        )

    for row in range(R):
        for d in range(1, n_mode):
            spread(d, row).start()

    def start_halo(d, side):
        @pl.when(has_left if side == 0 else has_right)
        def _():
            halo(d, side).start()

    start_halo(0, 0)
    start_halo(0, 1)
    for r in range(R):
        fields[1 + r][me] = x_ref[r]

    @pl.when(jnp.logical_not(has_left))
    def _():
        for g in range(n_mode):
            fields[0][g] = jnp.zeros_like(fields[0][g])

    @pl.when(jnp.logical_not(has_right))
    def _():
        for g in range(n_mode):
            fields[R + 1][g] = jnp.zeros_like(fields[R + 1][g])

    load_metric.wait()
    load_plan.wait()

    def arrive(row):
        for d in range(1, n_mode):
            spread(d, row).wait_recv()
            if row == 0:
                start_halo(d, 0)
            if row == R - 1:
                start_halo(d, 1)

    def arrive_halo():
        for d in range(n_mode):
            @pl.when(has_right)
            def _():
                halo(d, 0).wait_recv()

            @pl.when(has_left)
            def _():
                halo(d, 1).wait_recv()

    lane = lax.rem(lax.broadcasted_iota(jnp.int32, (half, width), 1), L)

    def prepare(r):
        for b in range(2):
            owner, which = plan_ref[0, b], plan_ref[1, b]
            block = fields[1 + r][owner, which].astype(F32)
            weight = metric_ref[2, r : r + 1, :]
            for c in range(2):
                scaled = block[:, c * L : (c + 1) * L] * weight
                movers[c, r, pl.ds(b * (half // jb), half // jb)] = scaled.reshape(
                    half // jb, jb, L
                )
        for b in range(2 // parts):
            source = 2 + b if parts == 1 else 2 + me
            owner, which = plan_ref[0, source], plan_ref[1, source]
            low = fields[r][owner, which].astype(F32)
            mid = fields[r + 1][owner, which].astype(F32)
            high = fields[r + 2][owner, which].astype(F32)
            first = jnp.concatenate([metric_ref[0, r : r + 1, :]] * C, axis=1)
            second = jnp.concatenate([metric_ref[1, r : r + 1, :]] * C, axis=1)
            after = jnp.where(lane == L - 1, 0.0, pltpu.roll(mid, width - 1, 1))
            before = jnp.where(lane == 0, 0.0, pltpu.roll(mid, 1, 1))
            place = slice(b * half, (b + 1) * half)
            slopes[0, r, place, :] = ((high - low) * first).astype(BF16).astype(F32)
            slopes[1, r, place, :] = ((after - before) * second).astype(BF16).astype(F32)
        if parts == 1:
            tests = x_ref[r].reshape(modes, width)
        else:
            tests = jnp.concatenate(
                [fields[1 + r][g].reshape(modes, width) for g in range(n_mode)], axis=0
            )
        weights[r] = tests.T

    tile = 16

    def project(q, some_rows, total=None):
        for r in some_rows:
            m = [
                [jnp.broadcast_to(movers[d, r, q, j : j + 1, :], (tile, L)) for j in range(jb)]
                for d in range(2)
            ]
            rows = []
            for k in range(0, own, tile):
                parted = [[] for _ in range(jb)]
                for c in range(C):
                    lanes = slice(c * L, (c + 1) * L)
                    s0 = slopes[0, r, k : k + tile, lanes]
                    s1 = slopes[1, r, k : k + tile, lanes]
                    for j in range(jb):
                        parted[j].append((m[0][j] * s0 + m[1][j] * s1).astype(BF16))
                rows += [jnp.concatenate(parted[j], axis=1) for j in range(jb)]
            part = jnp.dot(
                jnp.concatenate(rows, axis=0), weights[r], preferred_element_type=F32
            )
            total = part if total is None else total + part
        return total

    def sort(total):
        order = [total[(k * jb + j) * tile : (k * jb + j + 1) * tile]
                 for j in range(jb) for k in range(own // tile)]
        return jnp.concatenate(order, axis=0)

    def pack(rows):
        h = rows.shape[0] // 2
        return jnp.concatenate([rows[:h], rows[h:]], axis=1)

    def to_twin(it):
        return remote(
            send1.at[it], recv1.at[it], s1_send.at[it], s1_recv.at[it], (me, twin)
        )

    def to_across(t):
        return remote(
            send2.at[t], recv2.at[t], s2_send.at[t], s2_recv.at[t], (me, across)
        )

    def to_along(t, e):
        return remote(
            send3.at[t, e], recv3.at[t, e], s3_send.at[t, e], s3_recv.at[t, e],
            (lax.rem(me + e, n_mode), along(t + 1)),
        )

    def columns(value):
        if parts == 1:
            return [value]
        low, high = pack(value[:, :modes]), pack(value[:, modes:])
        return [jnp.where(me == 0, low, high), jnp.where(me == 0, high, low)]

    def gathered(it):
        to_twin(it).wait_recv()
        return keep[it] + recv1[it].astype(F32)

    def step(it, carry):
        t = lax.rem(it, nz)
        column = jnp.where(it < nz, 1 - y, y)
        q = lax.rem(z + 1 + t, nz) * 2 + column
        total = sort(project(q, (0, R - 1), partial[q]))
        rows = total.shape[0] // 2
        low, high = total[:rows], total[rows:]
        if parts == 1:
            low, high = pack(low), pack(high)
        keep[it] = jnp.where(core == 0, low, high)
        send1[it] = jnp.where(core == 0, high, low).astype(BF16)
        to_twin(it).start()

        @pl.when((it >= 1) & (it <= nz))
        def _():
            t = it - 1
            send2[t] = gathered(it - 1).astype(BF16)
            to_across(t).start()

        @pl.when(it > nz)
        def _():
            t = it - 1 - nz
            value = gathered(it - 1)
            to_across(t).wait_recv()
            for e, piece in enumerate(columns(value + recv2[t].astype(F32))):
                send3[t, e] = piece.astype(BF16)
                to_along(t, e).start()

        return carry

    inner = range(1, R - 1)
    for r in range(R):
        arrive(r)
        ready = [r - 1] if r - 1 in inner else []
        for i in ready:
            prepare(i)

            @pl.loop(0, nq)
            def _(q):
                partial[q] = project(q, (i,), partial[q] if i > 1 else None)

    arrive_halo()
    prepare(0)
    prepare(R - 1)
    lax.fori_loop(0, nq, step, 0)

    value = gathered(nq - 1)
    to_across(nz - 1).wait_recv()
    pieces = columns(value + recv2[nz - 1].astype(F32))
    if parts == 2:
        send3[nz - 1, 1] = pieces[1].astype(BF16)
        to_along(nz - 1, 1).start()
    for e in range(parts):
        value = pieces[0] if e == 0 else None
        for t in range(nz if e else nz - 1):
            to_along(t, e).wait_recv()
            got = recv3[t, e].astype(F32)
            value = got if value is None else value + got
        value = value * norm_factor
        halves = [value[:, :modes], value[:, modes:]]
        if parts == 1:
            h = value.shape[0]
            result[pl.ds(0, h), :] = halves[0]
            result[pl.ds(h, h), :] = halves[1]
        else:
            value = jnp.concatenate(halves, axis=0)
            column = me if e == 0 else 1 - me
            for j in range(value.shape[0] // own):
                start = pl.multiple_of(j * modes + column * own, own)
                result[pl.ds(start, own), :] = value[j * own : (j + 1) * own]

    out_ref[...] = result[...].T

    for d in range(1, n_mode):
        for row in range(R):
            spread(d, row).wait_send()
    for d in range(n_mode):
        @pl.when(has_left)
        def _():
            halo(d, 0).wait_send()

        @pl.when(has_right)
        def _():
            halo(d, 1).wait_send()
    for it in range(nq):
        to_twin(it).wait_send()
    for t in range(nz):
        to_across(t).wait_send()
    for t in range(nz):
        for e in range(parts):
            if t < nz - 1 or e > 0:
                to_along(t, e).wait_send()


def body(mode_fields, metric, plan):
    n_mode, n = lax.axis_size("mode"), lax.axis_size("space")
    modes, C, R, L = mode_fields.shape
    half, width = modes // 2, C * L
    norm_factor = float(R * n * L) ** (-0.5)
    out_rows = modes * modes // n
    h = out_rows // 2
    nq, nz = n // 2, n // 4
    jb = modes // nq
    parts = 2 if n_mode == 2 else 1
    x = mode_fields.transpose(2, 0, 1, 3).reshape(R, 2, half, width)
    dma = pltpu.SemaphoreType.DMA
    return pl.pallas_call(
        functools.partial(kernel, n_mode, n, parts, norm_factor),
        out_shape=jax.ShapeDtypeStruct((modes, out_rows), F32),
        in_specs=[
            pl.BlockSpec(memory_space=pltpu.VMEM),
            pl.BlockSpec(memory_space=pltpu.HBM),
            pl.BlockSpec(memory_space=pltpu.HBM),
        ],
        out_specs=pl.BlockSpec(memory_space=pltpu.VMEM),
        scratch_shapes=[
            pltpu.VMEM(metric.shape, F32),
            pltpu.SMEM(plan.shape[::-1], jnp.int32),
            pltpu.VMEM((out_rows, modes), F32),
            pltpu.VMEM((nq, jb * modes // parts, modes * parts), F32),
            pltpu.VMEM((R, width, modes * parts), BF16),
            pltpu.VMEM((2, R, modes // parts, width), F32),
            pltpu.VMEM((2, R, nq, jb, L), F32),
            pltpu.VMEM((nq, h, 2 * modes), F32),
            pltpu.VMEM((nq, h, 2 * modes), BF16),
            pltpu.VMEM((nq, h, 2 * modes), BF16),
            pltpu.VMEM((nz, h, 2 * modes), BF16),
            pltpu.VMEM((nz, h, 2 * modes), BF16),
            pltpu.VMEM((nz, parts, h // parts, 2 * modes), BF16),
            pltpu.VMEM((nz, parts, h // parts, 2 * modes), BF16),
            dma((2,)),
            dma((n_mode, R)),
            dma((n_mode, R)),
            dma((n_mode, 2)),
            dma((n_mode, 2)),
            dma((nq,)),
            dma((nq,)),
            dma((nz,)),
            dma((nz,)),
            dma((nz, parts)),
            dma((nz, parts)),
            *[pltpu.VMEM((n_mode, 2, half, width), BF16) for _ in range(R + 2)],
        ],
        compiler_params=pltpu.CompilerParams(
            collective_id=0, has_side_effects=True, vmem_limit_bytes=40 * 1024 * 1024
        ),
    )(x, metric, plan.T).T


def solution(mesh):
    return jax.shard_map(
        body,
        mesh=mesh,
        in_specs=(P("mode", None, "space", None), P(None, "space", None), P()),
        out_specs=P("space", "mode"),
        check_vma=False,
    )
```

```python
import functools

import jax
import jax.numpy as jnp
from jax import lax
from jax.experimental import pallas as pl
from jax.experimental.pallas import tpu as pltpu
from jax.sharding import PartitionSpec as P

MESH = pl.DeviceIdType.MESH
F32 = jnp.float32
BF16 = jnp.bfloat16


def kernel(
    n_mode, n, parts, norm_factor,
    x_ref, metric_hbm, plan_hbm, out_ref,
    metric_ref, plan_ref, result, weights, slopes, movers, keep, send1, recv1, send2, recv2, send3, recv3,
    load_sem, x_send, x_recv, h_send, h_recv, s1_send, s1_recv, s2_send, s2_recv, s3_send, s3_recv, *fields,
):
    R, _, half, width = x_ref.shape
    modes = 2 * half
    own = modes // parts
    L = metric_ref.shape[2]
    C = width // L
    nq, nz = n // 2, n // 4
    jb = movers.shape[3]

    me = lax.axis_index("mode")
    s = lax.axis_index("space")
    core = lax.rem(s, 2)
    pair = s // 2
    y = lax.rem(pair, 2)
    z = pair // 2
    twin = s + 1 - 2 * core
    across = s + 2 - 4 * y
    has_left = s > 0
    has_right = s < n - 1
    has_other = ((core == 1) & has_right) | ((core == 0) & has_left)
    other = jnp.clip(s + 2 * core - 1, 0, n - 1)

    def along(step):
        return (lax.rem(z + step, nz) * 2 + y) * 2 + core

    load_metric = pltpu.make_async_copy(metric_hbm, metric_ref, load_sem.at[0])
    load_plan = pltpu.make_async_copy(plan_hbm, plan_ref, load_sem.at[1])
    load_metric.start()
    load_plan.start()

    barrier = pltpu.get_barrier_semaphore()

    def greet(device):
        pl.semaphore_signal(barrier, inc=1, device_id=device, device_id_type=MESH)

    for d in range(1, n_mode):
        greet((lax.rem(me + d, n_mode), s))
    greet((me, twin))
    greet((me, across))
    for step in range(1, nz):
        for e in range(parts):
            greet((lax.rem(me + e, n_mode), along(step)))

    @pl.when(has_other)
    def _():
        greet((me, other))

    greeted = (n_mode - 1) + 2 + parts * (nz - 1)
    pl.semaphore_wait(barrier, jnp.where(has_other, greeted + 1, greeted))

    def remote(src, dst, send, recv, device):
        return pltpu.make_async_remote_copy(
            src_ref=src, dst_ref=dst, send_sem=send, recv_sem=recv,
            device_id=device, device_id_type=MESH,
        )

    def spread(d, row):
        return remote(
            x_ref.at[row], fields[1 + row].at[me],
            x_send.at[d, row], x_recv.at[d, row], (lax.rem(me + d, n_mode), s),
        )

    def halo(d, side):
        group = lax.rem(me + n_mode - d, n_mode)
        if d == 0:
            src = x_ref.at[0 if side == 0 else R - 1]
        else:
            src = fields[1 if side == 0 else R].at[group]
        target = (me, jnp.maximum(s - 1, 0)) if side == 0 else (me, jnp.minimum(s + 1, n - 1))
        return remote(
            src, fields[R + 1 if side == 0 else 0].at[group],
            h_send.at[d, side], h_recv.at[d, side], target,
        )

    arrivals = [0, R - 1] + list(range(1, R - 1))
    for row in arrivals:
        for d in range(1, n_mode):
            spread(d, row).start()

    def start_halo(d, side):
        @pl.when(has_left if side == 0 else has_right)
        def _():
            halo(d, side).start()

    start_halo(0, 0)
    start_halo(0, 1)
    for r in range(R):
        fields[1 + r][me] = x_ref[r]

    @pl.when(jnp.logical_not(has_left))
    def _():
        for g in range(n_mode):
            fields[0][g] = jnp.zeros_like(fields[0][g])

    @pl.when(jnp.logical_not(has_right))
    def _():
        for g in range(n_mode):
            fields[R + 1][g] = jnp.zeros_like(fields[R + 1][g])

    load_metric.wait()
    load_plan.wait()

    def arrive(row):
        for d in range(1, n_mode):
            spread(d, row).wait_recv()
            if row == 0:
                start_halo(d, 0)
            if row == R - 1:
                start_halo(d, 1)

    def arrive_halo():
        for d in range(n_mode):
            @pl.when(has_right)
            def _():
                halo(d, 0).wait_recv()

            @pl.when(has_left)
            def _():
                halo(d, 1).wait_recv()

    lane = lax.rem(lax.broadcasted_iota(jnp.int32, (half, width), 1), L)

    def prepare(r):
        for b in range(2):
            owner, which = plan_ref[0, b], plan_ref[1, b]
            block = fields[1 + r][owner, which].astype(F32)
            weight = metric_ref[2, r : r + 1, :]
            for c in range(2):
                scaled = block[:, c * L : (c + 1) * L] * weight
                movers[c, r, pl.ds(b * (half // jb), half // jb)] = scaled.reshape(
                    half // jb, jb, L
                )
        for b in range(2 // parts):
            source = 2 + b if parts == 1 else 2 + me
            owner, which = plan_ref[0, source], plan_ref[1, source]
            low = fields[r][owner, which].astype(F32)
            mid = fields[r + 1][owner, which].astype(F32)
            high = fields[r + 2][owner, which].astype(F32)
            first = jnp.concatenate([metric_ref[0, r : r + 1, :]] * C, axis=1)
            second = jnp.concatenate([metric_ref[1, r : r + 1, :]] * C, axis=1)
            after = jnp.where(lane == L - 1, 0.0, pltpu.roll(mid, width - 1, 1))
            before = jnp.where(lane == 0, 0.0, pltpu.roll(mid, 1, 1))
            place = slice(b * half, (b + 1) * half)
            slopes[0, r, place, :] = ((high - low) * first).astype(BF16).astype(F32)
            slopes[1, r, place, :] = ((after - before) * second).astype(BF16).astype(F32)

    def weigh(r):
        if parts == 1:
            tests = x_ref[r].reshape(modes, width)
        else:
            tests = jnp.concatenate(
                [fields[1 + r][g].reshape(modes, width) for g in range(n_mode)], axis=0
            )
        weights[r] = tests.T

    tile = 16

    def project(q, some_rows, total=None):
        for r in some_rows:
            m = [
                [jnp.broadcast_to(movers[d, r, q, j : j + 1, :], (tile, L)) for j in range(jb)]
                for d in range(2)
            ]
            rows = []
            for k in range(0, own, tile):
                parted = [[] for _ in range(jb)]
                for c in range(C):
                    lanes = slice(c * L, (c + 1) * L)
                    s0 = slopes[0, r, k : k + tile, lanes]
                    s1 = slopes[1, r, k : k + tile, lanes]
                    for j in range(jb):
                        parted[j].append((m[0][j] * s0 + m[1][j] * s1).astype(BF16))
                rows += [jnp.concatenate(parted[j], axis=1) for j in range(jb)]
            part = jnp.dot(
                jnp.concatenate(rows, axis=0), weights[r], preferred_element_type=F32
            )
            total = part if total is None else total + part
        return total

    def sort(total):
        order = [total[(k * jb + j) * tile : (k * jb + j + 1) * tile]
                 for j in range(jb) for k in range(own // tile)]
        return jnp.concatenate(order, axis=0)

    def pack(rows):
        h = rows.shape[0] // 2
        return jnp.concatenate([rows[:h], rows[h:]], axis=1)

    def to_twin(it):
        return remote(
            send1.at[it], recv1.at[it], s1_send.at[it], s1_recv.at[it], (me, twin)
        )

    def to_across(t):
        return remote(
            send2.at[t], recv2.at[t], s2_send.at[t], s2_recv.at[t], (me, across)
        )

    def to_along(t, e):
        return remote(
            send3.at[t, e], recv3.at[t, e], s3_send.at[t, e], s3_recv.at[t, e],
            (lax.rem(me + e, n_mode), along(t + 1)),
        )

    def columns(value):
        if parts == 1:
            return [value]
        low, high = pack(value[:, :modes]), pack(value[:, modes:])
        return [jnp.where(me == 0, low, high), jnp.where(me == 0, high, low)]

    def gathered(it):
        to_twin(it).wait_recv()
        return keep[it] + recv1[it].astype(F32)

    def place(it):
        even = (lax.rem(it, 2) == 0) & (it > 0)
        t = jnp.where(even, it // 2 - 1, jnp.minimum((it + 1) // 2, nz - 1))
        return even | (it == nq - 1), t

    def step(it, carry):
        mine, t = place(it)
        column = jnp.where(mine, y, 1 - y)
        q = lax.rem(z + 1 + t, nz) * 2 + column
        total = sort(project(q, range(R)))
        rows = total.shape[0] // 2
        low, high = total[:rows], total[rows:]
        if parts == 1:
            low, high = pack(low), pack(high)
        keep[it] = jnp.where(core == 0, low, high)
        send1[it] = jnp.where(core == 0, high, low).astype(BF16)
        to_twin(it).start()

        before, last = place(it - 1)

        @pl.when((it >= 1) & jnp.logical_not(before))
        def _():
            send2[last] = gathered(it - 1).astype(BF16)
            to_across(last).start()

        @pl.when((it >= 1) & before)
        def _():
            value = gathered(it - 1)
            to_across(last).wait_recv()
            for e, piece in enumerate(columns(value + recv2[last].astype(F32))):
                send3[last, e] = piece.astype(BF16)
                to_along(last, e).start()

        return carry

    for r in arrivals:
        arrive(r)
        weigh(r)
    for r in range(1, R - 1):
        prepare(r)
    arrive_halo()
    prepare(0)
    prepare(R - 1)
    lax.fori_loop(0, nq, step, 0)

    value = gathered(nq - 1)
    to_across(nz - 1).wait_recv()
    pieces = columns(value + recv2[nz - 1].astype(F32))
    if parts == 2:
        send3[nz - 1, 1] = pieces[1].astype(BF16)
        to_along(nz - 1, 1).start()
    for e in range(parts):
        value = pieces[0] if e == 0 else None
        for t in range(nz if e else nz - 1):
            to_along(t, e).wait_recv()
            got = recv3[t, e].astype(F32)
            value = got if value is None else value + got
        value = value * norm_factor
        halves = [value[:, :modes], value[:, modes:]]
        if parts == 1:
            h = value.shape[0]
            result[pl.ds(0, h), :] = halves[0]
            result[pl.ds(h, h), :] = halves[1]
        else:
            value = jnp.concatenate(halves, axis=0)
            column = me if e == 0 else 1 - me
            for j in range(value.shape[0] // own):
                start = pl.multiple_of(j * modes + column * own, own)
                result[pl.ds(start, own), :] = value[j * own : (j + 1) * own]

    out_ref[...] = result[...].T

    for d in range(1, n_mode):
        for row in range(R):
            spread(d, row).wait_send()
    for d in range(n_mode):
        @pl.when(has_left)
        def _():
            halo(d, 0).wait_send()

        @pl.when(has_right)
        def _():
            halo(d, 1).wait_send()
    for it in range(nq):
        to_twin(it).wait_send()
    for t in range(nz):
        to_across(t).wait_send()
    for t in range(nz):
        for e in range(parts):
            if t < nz - 1 or e > 0:
                to_along(t, e).wait_send()


def body(mode_fields, metric, plan):
    n_mode, n = lax.axis_size("mode"), lax.axis_size("space")
    modes, C, R, L = mode_fields.shape
    half, width = modes // 2, C * L
    norm_factor = float(R * n * L) ** (-0.5)
    out_rows = modes * modes // n
    h = out_rows // 2
    nq, nz = n // 2, n // 4
    jb = modes // nq
    parts = 2 if n_mode == 2 else 1
    x = mode_fields.transpose(2, 0, 1, 3).reshape(R, 2, half, width)
    dma = pltpu.SemaphoreType.DMA
    return pl.pallas_call(
        functools.partial(kernel, n_mode, n, parts, norm_factor),
        out_shape=jax.ShapeDtypeStruct((modes, out_rows), F32),
        in_specs=[
            pl.BlockSpec(memory_space=pltpu.VMEM),
            pl.BlockSpec(memory_space=pltpu.HBM),
            pl.BlockSpec(memory_space=pltpu.HBM),
        ],
        out_specs=pl.BlockSpec(memory_space=pltpu.VMEM),
        scratch_shapes=[
            pltpu.VMEM(metric.shape, F32),
            pltpu.SMEM(plan.shape[::-1], jnp.int32),
            pltpu.VMEM((out_rows, modes), F32),
            pltpu.VMEM((R, width, modes * parts), BF16),
            pltpu.VMEM((2, R, modes // parts, width), F32),
            pltpu.VMEM((2, R, nq, jb, L), F32),
            pltpu.VMEM((nq, h, 2 * modes), F32),
            pltpu.VMEM((nq, h, 2 * modes), BF16),
            pltpu.VMEM((nq, h, 2 * modes), BF16),
            pltpu.VMEM((nz, h, 2 * modes), BF16),
            pltpu.VMEM((nz, h, 2 * modes), BF16),
            pltpu.VMEM((nz, parts, h // parts, 2 * modes), BF16),
            pltpu.VMEM((nz, parts, h // parts, 2 * modes), BF16),
            dma((2,)),
            dma((n_mode, R)),
            dma((n_mode, R)),
            dma((n_mode, 2)),
            dma((n_mode, 2)),
            dma((nq,)),
            dma((nq,)),
            dma((nz,)),
            dma((nz,)),
            dma((nz, parts)),
            dma((nz, parts)),
            *[pltpu.VMEM((n_mode, 2, half, width), BF16) for _ in range(R + 2)],
        ],
        compiler_params=pltpu.CompilerParams(
            collective_id=0, has_side_effects=True, vmem_limit_bytes=40 * 1024 * 1024
        ),
    )(x, metric, plan.T).T


def solution(mesh):
    return jax.shard_map(
        body,
        mesh=mesh,
        in_specs=(P("mode", None, "space", None), P(None, "space", None), P()),
        out_specs=P("space", "mode"),
        check_vma=False,
    )
```

```python
import functools

import jax
import jax.numpy as jnp
from jax import lax
from jax.experimental import pallas as pl
from jax.experimental.pallas import tpu as pltpu
from jax.sharding import PartitionSpec as P

MESH = pl.DeviceIdType.MESH
F32 = jnp.float32
BF16 = jnp.bfloat16


def kernel(
    n_mode, n, parts, norm_factor,
    x_ref, metric_hbm, plan_hbm, out_ref,
    metric_ref, plan_ref, result, weights, slopes, movers, keep, send1, recv1, send2, recv2, send3, recv3,
    load_sem, x_send, x_recv, h_send, h_recv, s1_send, s1_recv, s2_send, s2_recv, s3_send, s3_recv, *fields,
):
    R, _, half, width = x_ref.shape
    modes = 2 * half
    own = modes // parts
    L = metric_ref.shape[2]
    C = width // L
    nq, nz = n // 2, n // 4
    jb = movers.shape[3]

    me = lax.axis_index("mode")
    s = lax.axis_index("space")
    core = lax.rem(s, 2)
    pair = s // 2
    y = lax.rem(pair, 2)
    z = pair // 2
    twin = s + 1 - 2 * core
    across = s + 2 - 4 * y
    has_left = s > 0
    has_right = s < n - 1
    has_other = ((core == 1) & has_right) | ((core == 0) & has_left)
    other = jnp.clip(s + 2 * core - 1, 0, n - 1)

    def along(step):
        return (lax.rem(z + step, nz) * 2 + y) * 2 + core

    load_metric = pltpu.make_async_copy(metric_hbm, metric_ref, load_sem.at[0])
    load_plan = pltpu.make_async_copy(plan_hbm, plan_ref, load_sem.at[1])
    load_metric.start()
    load_plan.start()

    barrier = pltpu.get_barrier_semaphore()

    def greet(device):
        pl.semaphore_signal(barrier, inc=1, device_id=device, device_id_type=MESH)

    for d in range(1, n_mode):
        greet((lax.rem(me + d, n_mode), s))
    greet((me, twin))
    greet((me, across))
    for step in range(1, nz):
        for e in range(parts):
            greet((lax.rem(me + e, n_mode), along(step)))

    @pl.when(has_other)
    def _():
        greet((me, other))

    greeted = (n_mode - 1) + 2 + parts * (nz - 1)
    pl.semaphore_wait(barrier, jnp.where(has_other, greeted + 1, greeted))

    def remote(src, dst, send, recv, device):
        return pltpu.make_async_remote_copy(
            src_ref=src, dst_ref=dst, send_sem=send, recv_sem=recv,
            device_id=device, device_id_type=MESH,
        )

    def spread(d, row):
        return remote(
            x_ref.at[row], fields[1 + row].at[me],
            x_send.at[d, row], x_recv.at[d, row], (lax.rem(me + d, n_mode), s),
        )

    def halo(d, side):
        group = lax.rem(me + n_mode - d, n_mode)
        if d == 0:
            src = x_ref.at[0 if side == 0 else R - 1]
        else:
            src = fields[1 if side == 0 else R].at[group]
        target = (me, jnp.maximum(s - 1, 0)) if side == 0 else (me, jnp.minimum(s + 1, n - 1))
        return remote(
            src, fields[R + 1 if side == 0 else 0].at[group],
            h_send.at[d, side], h_recv.at[d, side], target,
        )

    arrivals = [0, R - 1] + list(range(1, R - 1))
    for row in arrivals:
        for d in range(1, n_mode):
            spread(d, row).start()

    def start_halo(d, side):
        @pl.when(has_left if side == 0 else has_right)
        def _():
            halo(d, side).start()

    start_halo(0, 0)
    start_halo(0, 1)
    for r in range(R):
        fields[1 + r][me] = x_ref[r]

    @pl.when(jnp.logical_not(has_left))
    def _():
        for g in range(n_mode):
            fields[0][g] = jnp.zeros_like(fields[0][g])

    @pl.when(jnp.logical_not(has_right))
    def _():
        for g in range(n_mode):
            fields[R + 1][g] = jnp.zeros_like(fields[R + 1][g])

    load_metric.wait()
    load_plan.wait()

    def arrive(row):
        for d in range(1, n_mode):
            spread(d, row).wait_recv()
            if row == 0:
                start_halo(d, 0)
            if row == R - 1:
                start_halo(d, 1)

    def arrive_halo():
        for d in range(n_mode):
            @pl.when(has_right)
            def _():
                halo(d, 0).wait_recv()

            @pl.when(has_left)
            def _():
                halo(d, 1).wait_recv()

    lane = lax.rem(lax.broadcasted_iota(jnp.int32, (half, width), 1), L)

    def prepare(r):
        for b in range(2):
            owner, which = plan_ref[0, b], plan_ref[1, b]
            block = fields[1 + r][owner, which].astype(F32)
            weight = metric_ref[2, r : r + 1, :]
            for c in range(2):
                scaled = block[:, c * L : (c + 1) * L] * weight
                movers[c, r, pl.ds(b * (half // jb), half // jb)] = scaled.reshape(
                    half // jb, jb, L
                )
        for b in range(2 // parts):
            source = 2 + b if parts == 1 else 2 + me
            owner, which = plan_ref[0, source], plan_ref[1, source]
            low = fields[r][owner, which].astype(F32)
            mid = fields[r + 1][owner, which].astype(F32)
            high = fields[r + 2][owner, which].astype(F32)
            first = jnp.concatenate([metric_ref[0, r : r + 1, :]] * C, axis=1)
            second = jnp.concatenate([metric_ref[1, r : r + 1, :]] * C, axis=1)
            after = jnp.where(lane == L - 1, 0.0, pltpu.roll(mid, width - 1, 1))
            before = jnp.where(lane == 0, 0.0, pltpu.roll(mid, 1, 1))
            place = slice(b * half, (b + 1) * half)
            slopes[0, r, place, :] = ((high - low) * first).astype(BF16).astype(F32)
            slopes[1, r, place, :] = ((after - before) * second).astype(BF16).astype(F32)

    def weigh(r):
        if parts == 1:
            tests = x_ref[r].reshape(modes, width)
        else:
            tests = jnp.concatenate(
                [fields[1 + r][g].reshape(modes, width) for g in range(n_mode)], axis=0
            )
        weights[r] = tests.T

    tile = 16

    def project(q, some_rows, total=None):
        for r in some_rows:
            m = [
                [jnp.broadcast_to(movers[d, r, q, j : j + 1, :], (tile, L)) for j in range(jb)]
                for d in range(2)
            ]
            rows = []
            for k in range(0, own, tile):
                parted = [[] for _ in range(jb)]
                for c in range(C):
                    lanes = slice(c * L, (c + 1) * L)
                    s0 = slopes[0, r, k : k + tile, lanes]
                    s1 = slopes[1, r, k : k + tile, lanes]
                    for j in range(jb):
                        parted[j].append((m[0][j] * s0 + m[1][j] * s1).astype(BF16))
                rows += [jnp.concatenate(parted[j], axis=1) for j in range(jb)]
            part = jnp.dot(
                jnp.concatenate(rows, axis=0), weights[r], preferred_element_type=F32
            )
            total = part if total is None else total + part
        return total

    def sort(total):
        order = [total[(k * jb + j) * tile : (k * jb + j + 1) * tile]
                 for j in range(jb) for k in range(own // tile)]
        return jnp.concatenate(order, axis=0)

    def pack(rows):
        h = rows.shape[0] // 2
        return jnp.concatenate([rows[:h], rows[h:]], axis=1)

    def to_twin(it):
        return remote(
            send1.at[it], recv1.at[it], s1_send.at[it], s1_recv.at[it], (me, twin)
        )

    def to_across(t):
        return remote(
            send2.at[t], recv2.at[t], s2_send.at[t], s2_recv.at[t], (me, across)
        )

    def to_along(t, e):
        return remote(
            send3.at[t, e], recv3.at[t, e], s3_send.at[t, e], s3_recv.at[t, e],
            (lax.rem(me + e, n_mode), along(t + 1)),
        )

    def columns(value):
        if parts == 1:
            return [value]
        low, high = pack(value[:, :modes]), pack(value[:, modes:])
        return [jnp.where(me == 0, low, high), jnp.where(me == 0, high, low)]

    def gathered(it):
        to_twin(it).wait_recv()
        return keep[it] + recv1[it].astype(F32)

    lag = min(3, nz)

    def forward_across(it):
        send2[it] = gathered(it).astype(BF16)
        to_across(it).start()

    def forward_along(it):
        t = it - nz
        value = gathered(it)
        to_across(t).wait_recv()
        for e, piece in enumerate(columns(value + recv2[t].astype(F32))):
            send3[t, e] = piece.astype(BF16)
            to_along(t, e).start()

    def step(it, carry):
        t = lax.rem(it, nz)
        column = jnp.where(it < nz, 1 - y, y)
        q = lax.rem(z + 1 + t, nz) * 2 + column
        total = sort(project(q, range(R)))
        rows = total.shape[0] // 2
        low, high = total[:rows], total[rows:]
        if parts == 1:
            low, high = pack(low), pack(high)
        keep[it] = jnp.where(core == 0, low, high)
        send1[it] = jnp.where(core == 0, high, low).astype(BF16)
        to_twin(it).start()

        @pl.when((it >= lag) & (it < lag + nz))
        def _():
            forward_across(it - lag)

        @pl.when(it >= lag + nz)
        def _():
            forward_along(it - lag)

        return carry

    for r in arrivals:
        arrive(r)
        weigh(r)
    for r in range(1, R - 1):
        prepare(r)
    arrive_halo()
    prepare(0)
    prepare(R - 1)
    lax.fori_loop(0, nq, step, 0)
    for it in range(nq - lag, nq - 1):
        forward_along(it)

    value = gathered(nq - 1)
    to_across(nz - 1).wait_recv()
    pieces = columns(value + recv2[nz - 1].astype(F32))
    if parts == 2:
        send3[nz - 1, 1] = pieces[1].astype(BF16)
        to_along(nz - 1, 1).start()
    for e in range(parts):
        value = pieces[0] if e == 0 else None
        for t in range(nz if e else nz - 1):
            to_along(t, e).wait_recv()
            got = recv3[t, e].astype(F32)
            value = got if value is None else value + got
        value = value * norm_factor
        halves = [value[:, :modes], value[:, modes:]]
        if parts == 1:
            h = value.shape[0]
            result[pl.ds(0, h), :] = halves[0]
            result[pl.ds(h, h), :] = halves[1]
        else:
            value = jnp.concatenate(halves, axis=0)
            column = me if e == 0 else 1 - me
            for j in range(value.shape[0] // own):
                start = pl.multiple_of(j * modes + column * own, own)
                result[pl.ds(start, own), :] = value[j * own : (j + 1) * own]

    out_ref[...] = result[...].T

    for d in range(1, n_mode):
        for row in range(R):
            spread(d, row).wait_send()
    for d in range(n_mode):
        @pl.when(has_left)
        def _():
            halo(d, 0).wait_send()

        @pl.when(has_right)
        def _():
            halo(d, 1).wait_send()
    for it in range(nq):
        to_twin(it).wait_send()
    for t in range(nz):
        to_across(t).wait_send()
    for t in range(nz):
        for e in range(parts):
            if t < nz - 1 or e > 0:
                to_along(t, e).wait_send()


def body(mode_fields, metric, plan):
    n_mode, n = lax.axis_size("mode"), lax.axis_size("space")
    modes, C, R, L = mode_fields.shape
    half, width = modes // 2, C * L
    norm_factor = float(R * n * L) ** (-0.5)
    out_rows = modes * modes // n
    h = out_rows // 2
    nq, nz = n // 2, n // 4
    jb = modes // nq
    parts = 2 if n_mode == 2 else 1
    x = mode_fields.transpose(2, 0, 1, 3).reshape(R, 2, half, width)
    dma = pltpu.SemaphoreType.DMA
    return pl.pallas_call(
        functools.partial(kernel, n_mode, n, parts, norm_factor),
        out_shape=jax.ShapeDtypeStruct((modes, out_rows), F32),
        in_specs=[
            pl.BlockSpec(memory_space=pltpu.VMEM),
            pl.BlockSpec(memory_space=pltpu.HBM),
            pl.BlockSpec(memory_space=pltpu.HBM),
        ],
        out_specs=pl.BlockSpec(memory_space=pltpu.VMEM),
        scratch_shapes=[
            pltpu.VMEM(metric.shape, F32),
            pltpu.SMEM(plan.shape[::-1], jnp.int32),
            pltpu.VMEM((out_rows, modes), F32),
            pltpu.VMEM((R, width, modes * parts), BF16),
            pltpu.VMEM((2, R, modes // parts, width), F32),
            pltpu.VMEM((2, R, nq, jb, L), F32),
            pltpu.VMEM((nq, h, 2 * modes), F32),
            pltpu.VMEM((nq, h, 2 * modes), BF16),
            pltpu.VMEM((nq, h, 2 * modes), BF16),
            pltpu.VMEM((nz, h, 2 * modes), BF16),
            pltpu.VMEM((nz, h, 2 * modes), BF16),
            pltpu.VMEM((nz, parts, h // parts, 2 * modes), BF16),
            pltpu.VMEM((nz, parts, h // parts, 2 * modes), BF16),
            dma((2,)),
            dma((n_mode, R)),
            dma((n_mode, R)),
            dma((n_mode, 2)),
            dma((n_mode, 2)),
            dma((nq,)),
            dma((nq,)),
            dma((nz,)),
            dma((nz,)),
            dma((nz, parts)),
            dma((nz, parts)),
            *[pltpu.VMEM((n_mode, 2, half, width), BF16) for _ in range(R + 2)],
        ],
        compiler_params=pltpu.CompilerParams(
            collective_id=0, has_side_effects=True, vmem_limit_bytes=40 * 1024 * 1024
        ),
    )(x, metric, plan.T).T


def solution(mesh):
    return jax.shard_map(
        body,
        mesh=mesh,
        in_specs=(P("mode", None, "space", None), P(None, "space", None), P()),
        out_specs=P("space", "mode"),
        check_vma=False,
    )
```

```python
import functools

import jax
import jax.numpy as jnp
from jax import lax
from jax.experimental import pallas as pl
from jax.experimental.pallas import tpu as pltpu
from jax.sharding import PartitionSpec as P

MESH = pl.DeviceIdType.MESH
F32 = jnp.float32
BF16 = jnp.bfloat16


def kernel(
    n_mode, n, parts, norm_factor,
    x_ref, metric_hbm, plan_hbm, out_ref,
    metric_ref, plan_ref, result, partial, weights, slopes, movers, keep, send1, recv1, send2, recv2, send3, recv3,
    load_sem, x_send, x_recv, h_send, h_recv, s1_send, s1_recv, s2_send, s2_recv, s3_send, s3_recv, *fields,
):
    R, C, _, half, L = x_ref.shape
    width = C * L
    modes = 2 * half
    own = modes // parts
    nq, nz = n // 2, n // 4
    jb = movers.shape[3]

    me = lax.axis_index("mode")
    s = lax.axis_index("space")
    core = lax.rem(s, 2)
    pair = s // 2
    y = lax.rem(pair, 2)
    z = pair // 2
    twin = s + 1 - 2 * core
    across = s + 2 - 4 * y
    has_left = s > 0
    has_right = s < n - 1
    has_other = ((core == 1) & has_right) | ((core == 0) & has_left)
    other = jnp.clip(s + 2 * core - 1, 0, n - 1)

    def along(step):
        return (lax.rem(z + step, nz) * 2 + y) * 2 + core

    load_metric = pltpu.make_async_copy(metric_hbm, metric_ref, load_sem.at[0])
    load_plan = pltpu.make_async_copy(plan_hbm, plan_ref, load_sem.at[1])
    load_metric.start()
    load_plan.start()

    barrier = pltpu.get_barrier_semaphore()

    def greet(device):
        pl.semaphore_signal(barrier, inc=1, device_id=device, device_id_type=MESH)

    for d in range(1, n_mode):
        greet((lax.rem(me + d, n_mode), s))
    greet((me, twin))
    greet((me, across))
    for step in range(1, nz):
        for e in range(parts):
            greet((lax.rem(me + e, n_mode), along(step)))

    @pl.when(has_other)
    def _():
        greet((me, other))

    greeted = (n_mode - 1) + 2 + parts * (nz - 1)
    pl.semaphore_wait(barrier, jnp.where(has_other, greeted + 1, greeted))

    def remote(src, dst, send, recv, device):
        return pltpu.make_async_remote_copy(
            src_ref=src, dst_ref=dst, send_sem=send, recv_sem=recv,
            device_id=device, device_id_type=MESH,
        )

    def spread(d, row):
        return remote(
            x_ref.at[row], fields[1 + row].at[me],
            x_send.at[d, row], x_recv.at[d, row], (lax.rem(me + d, n_mode), s),
        )

    def halo(d, side):
        group = lax.rem(me + n_mode - d, n_mode)
        if d == 0:
            src = x_ref.at[0 if side == 0 else R - 1]
        else:
            src = fields[1 if side == 0 else R].at[group]
        target = (me, jnp.maximum(s - 1, 0)) if side == 0 else (me, jnp.minimum(s + 1, n - 1))
        return remote(
            src, fields[R + 1 if side == 0 else 0].at[group],
            h_send.at[d, side], h_recv.at[d, side], target,
        )

    arrivals = [0, R - 1] + list(range(1, R - 1))
    for row in arrivals:
        for d in range(1, n_mode):
            spread(d, row).start()

    def start_halo(d, side):
        @pl.when(has_left if side == 0 else has_right)
        def _():
            halo(d, side).start()

    start_halo(0, 0)
    start_halo(0, 1)
    for r in range(R):
        fields[1 + r][me] = x_ref[r]

    @pl.when(jnp.logical_not(has_left))
    def _():
        for g in range(n_mode):
            fields[0][g] = jnp.zeros_like(fields[0][g])

    @pl.when(jnp.logical_not(has_right))
    def _():
        for g in range(n_mode):
            fields[R + 1][g] = jnp.zeros_like(fields[R + 1][g])

    load_metric.wait()
    load_plan.wait()

    def arrive(row):
        for d in range(1, n_mode):
            spread(d, row).wait_recv()
            if row == 0:
                start_halo(d, 0)
            if row == R - 1:
                start_halo(d, 1)

    def arrive_halo():
        for d in range(n_mode):
            @pl.when(has_right)
            def _():
                halo(d, 0).wait_recv()

            @pl.when(has_left)
            def _():
                halo(d, 1).wait_recv()

    lane = lax.broadcasted_iota(jnp.int32, (half, L), 1)

    def prepare(r):
        first, second, weight = (metric_ref[i, r : r + 1, :] for i in range(3))
        for b in range(2):
            owner, which = plan_ref[0, b], plan_ref[1, b]
            for c in range(2):
                scaled = fields[1 + r][owner, c, which].astype(F32) * weight
                movers[c, r, pl.ds(b * (half // jb), half // jb)] = scaled.reshape(
                    half // jb, jb, L
                )
        for b in range(2 // parts):
            source = 2 + b if parts == 1 else 2 + me
            owner, which = plan_ref[0, source], plan_ref[1, source]
            rows = slice(b * half, (b + 1) * half)
            for c in range(C):
                lanes = slice(c * L, (c + 1) * L)
                low = fields[r][owner, c, which].astype(F32)
                mid = fields[r + 1][owner, c, which].astype(F32)
                high = fields[r + 2][owner, c, which].astype(F32)
                after = jnp.where(lane == L - 1, 0.0, pltpu.roll(mid, L - 1, 1))
                before = jnp.where(lane == 0, 0.0, pltpu.roll(mid, 1, 1))
                slopes[0, r, rows, lanes] = ((high - low) * first).astype(BF16).astype(F32)
                slopes[1, r, rows, lanes] = ((after - before) * second).astype(BF16).astype(F32)

    def weigh(r):
        for c in range(C):
            if parts == 1:
                tests = x_ref[r, c].reshape(modes, L)
            else:
                tests = jnp.concatenate(
                    [fields[1 + r][g, c].reshape(modes, L) for g in range(n_mode)], axis=0
                )
            weights[r, c * L : (c + 1) * L, :] = tests.T

    tile = 16

    def project(q, some_rows, total=None):
        for r in some_rows:
            m = [
                [jnp.broadcast_to(movers[d, r, q, j : j + 1, :], (tile, L)) for j in range(jb)]
                for d in range(2)
            ]
            rows = []
            for k in range(0, own, tile):
                parted = [[] for _ in range(jb)]
                for c in range(C):
                    lanes = slice(c * L, (c + 1) * L)
                    s0 = slopes[0, r, k : k + tile, lanes]
                    s1 = slopes[1, r, k : k + tile, lanes]
                    for j in range(jb):
                        parted[j].append((m[0][j] * s0 + m[1][j] * s1).astype(BF16))
                rows += [jnp.concatenate(parted[j], axis=1) for j in range(jb)]
            part = jnp.dot(
                jnp.concatenate(rows, axis=0), weights[r], preferred_element_type=F32
            )
            total = part if total is None else total + part
        return total

    def sort(total):
        order = [total[(k * jb + j) * tile : (k * jb + j + 1) * tile]
                 for j in range(jb) for k in range(own // tile)]
        return jnp.concatenate(order, axis=0)

    def pack(rows):
        h = rows.shape[0] // 2
        return jnp.concatenate([rows[:h], rows[h:]], axis=1)

    def to_twin(it):
        return remote(
            send1.at[it], recv1.at[it], s1_send.at[it], s1_recv.at[it], (me, twin)
        )

    def to_across(t):
        return remote(
            send2.at[t], recv2.at[t], s2_send.at[t], s2_recv.at[t], (me, across)
        )

    def to_along(t, e):
        return remote(
            send3.at[t, e], recv3.at[t, e], s3_send.at[t, e], s3_recv.at[t, e],
            (lax.rem(me + e, n_mode), along(t + 1)),
        )

    def columns(value):
        if parts == 1:
            return [value]
        low, high = pack(value[:, :modes]), pack(value[:, modes:])
        return [jnp.where(me == 0, low, high), jnp.where(me == 0, high, low)]

    def gathered(it):
        to_twin(it).wait_recv()
        return keep[it] + recv1[it].astype(F32)

    lag = min(3, nz)

    def forward_across(it):
        send2[it] = gathered(it).astype(BF16)
        to_across(it).start()

    def forward_along(it):
        t = it - nz
        value = gathered(it)
        to_across(t).wait_recv()
        for e, piece in enumerate(columns(value + recv2[t].astype(F32))):
            send3[t, e] = piece.astype(BF16)
            to_along(t, e).start()

    def step(it, carry):
        t = lax.rem(it, nz)
        column = jnp.where(it < nz, 1 - y, y)
        q = lax.rem(z + 1 + t, nz) * 2 + column
        total = sort(project(q, (0, R - 1), partial[q]))
        rows = total.shape[0] // 2
        low, high = total[:rows], total[rows:]
        if parts == 1:
            low, high = pack(low), pack(high)
        keep[it] = jnp.where(core == 0, low, high)
        send1[it] = jnp.where(core == 0, high, low).astype(BF16)
        to_twin(it).start()

        @pl.when((it >= lag) & (it < lag + nz))
        def _():
            forward_across(it - lag)

        @pl.when(it >= lag + nz)
        def _():
            forward_along(it - lag)

        return carry

    for r in arrivals:
        arrive(r)
        weigh(r)
    for r in range(1, R - 1):
        prepare(r)

    @pl.loop(0, nq)
    def _(q):
        partial[q] = project(q, range(1, R - 1))

    arrive_halo()
    prepare(0)
    prepare(R - 1)
    lax.fori_loop(0, nq, step, 0)
    for it in range(nq - lag, nq - 1):
        forward_along(it)

    value = gathered(nq - 1)
    to_across(nz - 1).wait_recv()
    pieces = columns(value + recv2[nz - 1].astype(F32))
    if parts == 2:
        send3[nz - 1, 1] = pieces[1].astype(BF16)
        to_along(nz - 1, 1).start()
    for e in range(parts):
        value = pieces[0] if e == 0 else None
        for t in range(nz if e else nz - 1):
            to_along(t, e).wait_recv()
            got = recv3[t, e].astype(F32)
            value = got if value is None else value + got
        value = value * norm_factor
        halves = [value[:, :modes], value[:, modes:]]
        if parts == 1:
            h = value.shape[0]
            result[pl.ds(0, h), :] = halves[0]
            result[pl.ds(h, h), :] = halves[1]
        else:
            value = jnp.concatenate(halves, axis=0)
            column = me if e == 0 else 1 - me
            for j in range(value.shape[0] // own):
                start = pl.multiple_of(j * modes + column * own, own)
                result[pl.ds(start, own), :] = value[j * own : (j + 1) * own]

    out_ref[...] = result[...].T

    for d in range(1, n_mode):
        for row in range(R):
            spread(d, row).wait_send()
    for d in range(n_mode):
        @pl.when(has_left)
        def _():
            halo(d, 0).wait_send()

        @pl.when(has_right)
        def _():
            halo(d, 1).wait_send()
    for it in range(nq):
        to_twin(it).wait_send()
    for t in range(nz):
        to_across(t).wait_send()
    for t in range(nz):
        for e in range(parts):
            if t < nz - 1 or e > 0:
                to_along(t, e).wait_send()


def body(mode_fields, metric, plan):
    n_mode, n = lax.axis_size("mode"), lax.axis_size("space")
    modes, C, R, L = mode_fields.shape
    half, width = modes // 2, C * L
    norm_factor = float(R * n * L) ** (-0.5)
    out_rows = modes * modes // n
    h = out_rows // 2
    nq, nz = n // 2, n // 4
    jb = modes // nq
    parts = 2 if n_mode == 2 else 1
    x = mode_fields.transpose(2, 1, 0, 3).reshape(R, C, 2, half, L)
    dma = pltpu.SemaphoreType.DMA
    return pl.pallas_call(
        functools.partial(kernel, n_mode, n, parts, norm_factor),
        out_shape=jax.ShapeDtypeStruct((modes, out_rows), F32),
        in_specs=[
            pl.BlockSpec(memory_space=pltpu.VMEM),
            pl.BlockSpec(memory_space=pltpu.HBM),
            pl.BlockSpec(memory_space=pltpu.HBM),
        ],
        out_specs=pl.BlockSpec(memory_space=pltpu.VMEM),
        scratch_shapes=[
            pltpu.VMEM(metric.shape, F32),
            pltpu.SMEM(plan.shape[::-1], jnp.int32),
            pltpu.VMEM((out_rows, modes), F32),
            pltpu.VMEM((nq, jb * modes // parts, modes * parts), F32),
            pltpu.VMEM((R, width, modes * parts), BF16),
            pltpu.VMEM((2, R, modes // parts, width), F32),
            pltpu.VMEM((2, R, nq, jb, L), F32),
            pltpu.VMEM((nq, h, 2 * modes), F32),
            pltpu.VMEM((nq, h, 2 * modes), BF16),
            pltpu.VMEM((nq, h, 2 * modes), BF16),
            pltpu.VMEM((nz, h, 2 * modes), BF16),
            pltpu.VMEM((nz, h, 2 * modes), BF16),
            pltpu.VMEM((nz, parts, h // parts, 2 * modes), BF16),
            pltpu.VMEM((nz, parts, h // parts, 2 * modes), BF16),
            dma((2,)),
            dma((n_mode, R)),
            dma((n_mode, R)),
            dma((n_mode, 2)),
            dma((n_mode, 2)),
            dma((nq,)),
            dma((nq,)),
            dma((nz,)),
            dma((nz,)),
            dma((nz, parts)),
            dma((nz, parts)),
            *[pltpu.VMEM((n_mode, C, 2, half, L), BF16) for _ in range(R + 2)],
        ],
        compiler_params=pltpu.CompilerParams(
            collective_id=0, has_side_effects=True, vmem_limit_bytes=40 * 1024 * 1024
        ),
    )(x, metric, plan.T).T


def solution(mesh):
    return jax.shard_map(
        body,
        mesh=mesh,
        in_specs=(P("mode", None, "space", None), P(None, "space", None), P()),
        out_specs=P("space", "mode"),
        check_vma=False,
    )
```

```python
import functools

import jax
import jax.numpy as jnp
from jax import lax
from jax.experimental import pallas as pl
from jax.experimental.pallas import tpu as pltpu
from jax.sharding import PartitionSpec as P

MESH = pl.DeviceIdType.MESH
F32 = jnp.float32
BF16 = jnp.bfloat16


def kernel(
    n_mode, n, parts, norm_factor,
    raw_ref, metric_hbm, plan_hbm, out_ref,
    metric_ref, plan_ref, result, x_ref, weights, slopes, movers, keep, send1, recv1, send2, recv2, send3, recv3,
    load_sem, x_send, x_recv, h_send, h_recv, s1_send, s1_recv, s2_send, s2_recv, s3_send, s3_recv, *fields,
):
    R, C, _, half, L = x_ref.shape
    width = C * L
    modes = 2 * half
    own = modes // parts
    nq, nz = n // 2, n // 4
    jb = movers.shape[3]

    me = lax.axis_index("mode")
    s = lax.axis_index("space")
    core = lax.rem(s, 2)
    pair = s // 2
    y = lax.rem(pair, 2)
    z = pair // 2
    twin = s + 1 - 2 * core
    across = s + 2 - 4 * y
    has_left = s > 0
    has_right = s < n - 1
    has_other = ((core == 1) & has_right) | ((core == 0) & has_left)
    other = jnp.clip(s + 2 * core - 1, 0, n - 1)

    def along(step):
        return (lax.rem(z + step, nz) * 2 + y) * 2 + core

    load_metric = pltpu.make_async_copy(metric_hbm, metric_ref, load_sem.at[0])
    load_plan = pltpu.make_async_copy(plan_hbm, plan_ref, load_sem.at[1])
    load_metric.start()
    load_plan.start()

    barrier = pltpu.get_barrier_semaphore()

    def greet(device):
        pl.semaphore_signal(barrier, inc=1, device_id=device, device_id_type=MESH)

    for d in range(1, n_mode):
        greet((lax.rem(me + d, n_mode), s))
    greet((me, twin))
    greet((me, across))
    for step in range(1, nz):
        for e in range(parts):
            greet((lax.rem(me + e, n_mode), along(step)))

    @pl.when(has_other)
    def _():
        greet((me, other))

    for c in range(C):
        turned = jnp.swapaxes(raw_ref[:, c].astype(F32), 0, 1)
        for r in range(R):
            x_ref[r, c] = turned[r].astype(BF16).reshape(2, half, L)

    greeted = (n_mode - 1) + 2 + parts * (nz - 1)
    pl.semaphore_wait(barrier, jnp.where(has_other, greeted + 1, greeted))

    def remote(src, dst, send, recv, device):
        return pltpu.make_async_remote_copy(
            src_ref=src, dst_ref=dst, send_sem=send, recv_sem=recv,
            device_id=device, device_id_type=MESH,
        )

    def spread(d, row):
        return remote(
            x_ref.at[row], fields[1 + row].at[me],
            x_send.at[d, row], x_recv.at[d, row], (lax.rem(me + d, n_mode), s),
        )

    def halo(d, side):
        group = lax.rem(me + n_mode - d, n_mode)
        if d == 0:
            src = x_ref.at[0 if side == 0 else R - 1]
        else:
            src = fields[1 if side == 0 else R].at[group]
        target = (me, jnp.maximum(s - 1, 0)) if side == 0 else (me, jnp.minimum(s + 1, n - 1))
        return remote(
            src, fields[R + 1 if side == 0 else 0].at[group],
            h_send.at[d, side], h_recv.at[d, side], target,
        )

    arrivals = [0, R - 1] + list(range(1, R - 1))
    for row in arrivals:
        for d in range(1, n_mode):
            spread(d, row).start()

    def start_halo(d, side):
        @pl.when(has_left if side == 0 else has_right)
        def _():
            halo(d, side).start()

    start_halo(0, 0)
    start_halo(0, 1)
    for r in range(R):
        fields[1 + r][me] = x_ref[r]

    @pl.when(jnp.logical_not(has_left))
    def _():
        for g in range(n_mode):
            fields[0][g] = jnp.zeros_like(fields[0][g])

    @pl.when(jnp.logical_not(has_right))
    def _():
        for g in range(n_mode):
            fields[R + 1][g] = jnp.zeros_like(fields[R + 1][g])

    load_metric.wait()
    load_plan.wait()

    def arrive(row):
        for d in range(1, n_mode):
            spread(d, row).wait_recv()
            if row == 0:
                start_halo(d, 0)
            if row == R - 1:
                start_halo(d, 1)

    def arrive_halo():
        for d in range(n_mode):
            @pl.when(has_right)
            def _():
                halo(d, 0).wait_recv()

            @pl.when(has_left)
            def _():
                halo(d, 1).wait_recv()

    lane = lax.broadcasted_iota(jnp.int32, (half, L), 1)

    def prepare(r):
        first, second, weight = (metric_ref[i, r : r + 1, :] for i in range(3))
        for b in range(2):
            owner, which = plan_ref[0, b], plan_ref[1, b]
            for c in range(2):
                scaled = fields[1 + r][owner, c, which].astype(F32) * weight
                movers[c, r, pl.ds(b * (half // jb), half // jb)] = scaled.reshape(
                    half // jb, jb, L
                )
        for b in range(2 // parts):
            source = 2 + b if parts == 1 else 2 + me
            owner, which = plan_ref[0, source], plan_ref[1, source]
            rows = slice(b * half, (b + 1) * half)
            for c in range(C):
                lanes = slice(c * L, (c + 1) * L)
                low = fields[r][owner, c, which].astype(F32)
                mid = fields[r + 1][owner, c, which].astype(F32)
                high = fields[r + 2][owner, c, which].astype(F32)
                after = jnp.where(lane == L - 1, 0.0, pltpu.roll(mid, L - 1, 1))
                before = jnp.where(lane == 0, 0.0, pltpu.roll(mid, 1, 1))
                slopes[0, r, rows, lanes] = ((high - low) * first).astype(BF16).astype(F32)
                slopes[1, r, rows, lanes] = ((after - before) * second).astype(BF16).astype(F32)

    def weigh(r):
        for c in range(C):
            if parts == 1:
                tests = x_ref[r, c].reshape(modes, L)
            else:
                tests = jnp.concatenate(
                    [fields[1 + r][g, c].reshape(modes, L) for g in range(n_mode)], axis=0
                )
            weights[r, c * L : (c + 1) * L, :] = tests.T

    tile = 16

    def project(q, some_rows, total=None):
        for r in some_rows:
            m = [
                [jnp.broadcast_to(movers[d, r, q, j : j + 1, :], (tile, L)) for j in range(jb)]
                for d in range(2)
            ]
            rows = []
            for k in range(0, own, tile):
                parted = [[] for _ in range(jb)]
                for c in range(C):
                    lanes = slice(c * L, (c + 1) * L)
                    s0 = slopes[0, r, k : k + tile, lanes]
                    s1 = slopes[1, r, k : k + tile, lanes]
                    for j in range(jb):
                        parted[j].append((m[0][j] * s0 + m[1][j] * s1).astype(BF16))
                rows += [jnp.concatenate(parted[j], axis=1) for j in range(jb)]
            part = jnp.dot(
                jnp.concatenate(rows, axis=0), weights[r], preferred_element_type=F32
            )
            total = part if total is None else total + part
        return total

    def sort(total):
        order = [total[(k * jb + j) * tile : (k * jb + j + 1) * tile]
                 for j in range(jb) for k in range(own // tile)]
        return jnp.concatenate(order, axis=0)

    def pack(rows):
        h = rows.shape[0] // 2
        return jnp.concatenate([rows[:h], rows[h:]], axis=1)

    def to_twin(it):
        return remote(
            send1.at[it], recv1.at[it], s1_send.at[it], s1_recv.at[it], (me, twin)
        )

    def to_across(t):
        return remote(
            send2.at[t], recv2.at[t], s2_send.at[t], s2_recv.at[t], (me, across)
        )

    def to_along(t, e):
        return remote(
            send3.at[t, e], recv3.at[t, e], s3_send.at[t, e], s3_recv.at[t, e],
            (lax.rem(me + e, n_mode), along(t + 1)),
        )

    def columns(value):
        if parts == 1:
            return [value]
        low, high = pack(value[:, :modes]), pack(value[:, modes:])
        return [jnp.where(me == 0, low, high), jnp.where(me == 0, high, low)]

    def gathered(it):
        to_twin(it).wait_recv()
        return keep[it] + recv1[it].astype(F32)

    lag = min(3, nz)

    def forward_across(it):
        send2[it] = gathered(it).astype(BF16)
        to_across(it).start()

    def forward_along(it):
        t = it - nz
        value = gathered(it)
        to_across(t).wait_recv()
        for e, piece in enumerate(columns(value + recv2[t].astype(F32))):
            send3[t, e] = piece.astype(BF16)
            to_along(t, e).start()

    def step(it, carry):
        t = lax.rem(it, nz)
        column = jnp.where(it < nz, 1 - y, y)
        q = lax.rem(z + 1 + t, nz) * 2 + column
        total = sort(project(q, range(R)))
        rows = total.shape[0] // 2
        low, high = total[:rows], total[rows:]
        if parts == 1:
            low, high = pack(low), pack(high)
        keep[it] = jnp.where(core == 0, low, high)
        send1[it] = jnp.where(core == 0, high, low).astype(BF16)
        to_twin(it).start()

        @pl.when((it >= lag) & (it < lag + nz))
        def _():
            forward_across(it - lag)

        @pl.when(it >= lag + nz)
        def _():
            forward_along(it - lag)

        return carry

    for r in arrivals:
        arrive(r)
        weigh(r)
    for r in range(1, R - 1):
        prepare(r)
    arrive_halo()
    prepare(0)
    prepare(R - 1)
    lax.fori_loop(0, nq, step, 0)
    for it in range(nq - lag, nq - 1):
        forward_along(it)

    value = gathered(nq - 1)
    to_across(nz - 1).wait_recv()
    pieces = columns(value + recv2[nz - 1].astype(F32))
    if parts == 2:
        send3[nz - 1, 1] = pieces[1].astype(BF16)
        to_along(nz - 1, 1).start()
    for e in range(parts):
        value = pieces[0] if e == 0 else None
        for t in range(nz if e else nz - 1):
            to_along(t, e).wait_recv()
            got = recv3[t, e].astype(F32)
            value = got if value is None else value + got
        value = value * norm_factor
        halves = [value[:, :modes], value[:, modes:]]
        if parts == 1:
            h = value.shape[0]
            result[pl.ds(0, h), :] = halves[0]
            result[pl.ds(h, h), :] = halves[1]
        else:
            value = jnp.concatenate(halves, axis=0)
            column = me if e == 0 else 1 - me
            for j in range(value.shape[0] // own):
                start = pl.multiple_of(j * modes + column * own, own)
                result[pl.ds(start, own), :] = value[j * own : (j + 1) * own]

    out_ref[...] = result[...].T

    for d in range(1, n_mode):
        for row in range(R):
            spread(d, row).wait_send()
    for d in range(n_mode):
        @pl.when(has_left)
        def _():
            halo(d, 0).wait_send()

        @pl.when(has_right)
        def _():
            halo(d, 1).wait_send()
    for it in range(nq):
        to_twin(it).wait_send()
    for t in range(nz):
        to_across(t).wait_send()
    for t in range(nz):
        for e in range(parts):
            if t < nz - 1 or e > 0:
                to_along(t, e).wait_send()


def body(mode_fields, metric, plan):
    n_mode, n = lax.axis_size("mode"), lax.axis_size("space")
    modes, C, R, L = mode_fields.shape
    half, width = modes // 2, C * L
    norm_factor = float(R * n * L) ** (-0.5)
    out_rows = modes * modes // n
    h = out_rows // 2
    nq, nz = n // 2, n // 4
    jb = modes // nq
    parts = 2 if n_mode == 2 else 1
    dma = pltpu.SemaphoreType.DMA
    return pl.pallas_call(
        functools.partial(kernel, n_mode, n, parts, norm_factor),
        out_shape=jax.ShapeDtypeStruct((modes, out_rows), F32),
        in_specs=[
            pl.BlockSpec(memory_space=pltpu.VMEM),
            pl.BlockSpec(memory_space=pltpu.HBM),
            pl.BlockSpec(memory_space=pltpu.HBM),
        ],
        out_specs=pl.BlockSpec(memory_space=pltpu.VMEM),
        scratch_shapes=[
            pltpu.VMEM(metric.shape, F32),
            pltpu.SMEM(plan.shape[::-1], jnp.int32),
            pltpu.VMEM((out_rows, modes), F32),
            pltpu.VMEM((R, C, 2, half, L), BF16),
            pltpu.VMEM((R, width, modes * parts), BF16),
            pltpu.VMEM((2, R, modes // parts, width), F32),
            pltpu.VMEM((2, R, nq, jb, L), F32),
            pltpu.VMEM((nq, h, 2 * modes), F32),
            pltpu.VMEM((nq, h, 2 * modes), BF16),
            pltpu.VMEM((nq, h, 2 * modes), BF16),
            pltpu.VMEM((nz, h, 2 * modes), BF16),
            pltpu.VMEM((nz, h, 2 * modes), BF16),
            pltpu.VMEM((nz, parts, h // parts, 2 * modes), BF16),
            pltpu.VMEM((nz, parts, h // parts, 2 * modes), BF16),
            dma((2,)),
            dma((n_mode, R)),
            dma((n_mode, R)),
            dma((n_mode, 2)),
            dma((n_mode, 2)),
            dma((nq,)),
            dma((nq,)),
            dma((nz,)),
            dma((nz,)),
            dma((nz, parts)),
            dma((nz, parts)),
            *[pltpu.VMEM((n_mode, C, 2, half, L), BF16) for _ in range(R + 2)],
        ],
        compiler_params=pltpu.CompilerParams(
            collective_id=0, has_side_effects=True, vmem_limit_bytes=40 * 1024 * 1024
        ),
    )(mode_fields, metric, plan.T).T


def solution(mesh):
    return jax.shard_map(
        body,
        mesh=mesh,
        in_specs=(P("mode", None, "space", None), P(None, "space", None), P()),
        out_specs=P("space", "mode"),
        check_vma=False,
    )
```

```python
import functools

import jax
import jax.numpy as jnp
from jax import lax
from jax.experimental import pallas as pl
from jax.experimental.pallas import tpu as pltpu
from jax.sharding import PartitionSpec as P

MESH = pl.DeviceIdType.MESH
F32 = jnp.float32
BF16 = jnp.bfloat16


def kernel(
    n_mode, n, parts, norm_factor,
    raw_hbm, metric_hbm, plan_hbm, out_ref,
    raw_ref, metric_ref, plan_ref, result, x_ref, weights, slopes, movers, keep, send1, recv1, send2, recv2, send3, recv3,
    load_sem, x_send, x_recv, h_send, h_recv, s1_send, s1_recv, s2_send, s2_recv, s3_send, s3_recv, *fields,
):
    R, C, _, half, L = x_ref.shape
    width = C * L
    modes = 2 * half
    own = modes // parts
    nq, nz = n // 2, n // 4
    jb = movers.shape[3]

    me = lax.axis_index("mode")
    s = lax.axis_index("space")
    core = lax.rem(s, 2)
    pair = s // 2
    y = lax.rem(pair, 2)
    z = pair // 2
    twin = s + 1 - 2 * core
    across = s + 2 - 4 * y
    has_left = s > 0
    has_right = s < n - 1
    has_other = ((core == 1) & has_right) | ((core == 0) & has_left)
    other = jnp.clip(s + 2 * core - 1, 0, n - 1)

    def along(step):
        return (lax.rem(z + step, nz) * 2 + y) * 2 + core

    load_metric = pltpu.make_async_copy(metric_hbm, metric_ref, load_sem.at[0])
    load_plan = pltpu.make_async_copy(plan_hbm, plan_ref, load_sem.at[1])
    load_raw = pltpu.make_async_copy(raw_hbm, raw_ref, load_sem.at[2])
    load_raw.start()
    load_metric.start()
    load_plan.start()

    barrier = pltpu.get_barrier_semaphore()

    def greet(device):
        pl.semaphore_signal(barrier, inc=1, device_id=device, device_id_type=MESH)

    for d in range(1, n_mode):
        greet((lax.rem(me + d, n_mode), s))
    greet((me, twin))
    greet((me, across))
    for step in range(1, nz):
        for e in range(parts):
            greet((lax.rem(me + e, n_mode), along(step)))

    @pl.when(has_other)
    def _():
        greet((me, other))

    load_raw.wait()
    for c in range(C):
        turned = jnp.swapaxes(raw_ref[:, c].astype(F32), 0, 1)
        for r in range(R):
            x_ref[r, c] = turned[r].astype(BF16).reshape(2, half, L)

    greeted = (n_mode - 1) + 2 + parts * (nz - 1)
    pl.semaphore_wait(barrier, jnp.where(has_other, greeted + 1, greeted))

    def remote(src, dst, send, recv, device):
        return pltpu.make_async_remote_copy(
            src_ref=src, dst_ref=dst, send_sem=send, recv_sem=recv,
            device_id=device, device_id_type=MESH,
        )

    def spread(d, row):
        return remote(
            x_ref.at[row], fields[1 + row].at[me],
            x_send.at[d, row], x_recv.at[d, row], (lax.rem(me + d, n_mode), s),
        )

    def halo(d, side):
        group = lax.rem(me + n_mode - d, n_mode)
        if d == 0:
            src = x_ref.at[0 if side == 0 else R - 1]
        else:
            src = fields[1 if side == 0 else R].at[group]
        target = (me, jnp.maximum(s - 1, 0)) if side == 0 else (me, jnp.minimum(s + 1, n - 1))
        return remote(
            src, fields[R + 1 if side == 0 else 0].at[group],
            h_send.at[d, side], h_recv.at[d, side], target,
        )

    arrivals = [0, R - 1] + list(range(1, R - 1))
    for row in arrivals:
        for d in range(1, n_mode):
            spread(d, row).start()

    def start_halo(d, side):
        @pl.when(has_left if side == 0 else has_right)
        def _():
            halo(d, side).start()

    start_halo(0, 0)
    start_halo(0, 1)
    for r in range(R):
        fields[1 + r][me] = x_ref[r]

    @pl.when(jnp.logical_not(has_left))
    def _():
        for g in range(n_mode):
            fields[0][g] = jnp.zeros_like(fields[0][g])

    @pl.when(jnp.logical_not(has_right))
    def _():
        for g in range(n_mode):
            fields[R + 1][g] = jnp.zeros_like(fields[R + 1][g])

    load_metric.wait()
    load_plan.wait()

    def arrive(row):
        for d in range(1, n_mode):
            spread(d, row).wait_recv()
            if row == 0:
                start_halo(d, 0)
            if row == R - 1:
                start_halo(d, 1)

    def arrive_halo():
        for d in range(n_mode):
            @pl.when(has_right)
            def _():
                halo(d, 0).wait_recv()

            @pl.when(has_left)
            def _():
                halo(d, 1).wait_recv()

    lane = lax.broadcasted_iota(jnp.int32, (half, L), 1)

    def prepare(r):
        first, second, weight = (metric_ref[i, r : r + 1, :] for i in range(3))
        for b in range(2):
            owner, which = plan_ref[0, b], plan_ref[1, b]
            for c in range(2):
                scaled = fields[1 + r][owner, c, which].astype(F32) * weight
                movers[c, r, pl.ds(b * (half // jb), half // jb)] = scaled.reshape(
                    half // jb, jb, L
                )
        for b in range(2 // parts):
            source = 2 + b if parts == 1 else 2 + me
            owner, which = plan_ref[0, source], plan_ref[1, source]
            rows = slice(b * half, (b + 1) * half)
            for c in range(C):
                lanes = slice(c * L, (c + 1) * L)
                low = fields[r][owner, c, which].astype(F32)
                mid = fields[r + 1][owner, c, which].astype(F32)
                high = fields[r + 2][owner, c, which].astype(F32)
                after = jnp.where(lane == L - 1, 0.0, pltpu.roll(mid, L - 1, 1))
                before = jnp.where(lane == 0, 0.0, pltpu.roll(mid, 1, 1))
                slopes[0, r, rows, lanes] = ((high - low) * first).astype(BF16).astype(F32)
                slopes[1, r, rows, lanes] = ((after - before) * second).astype(BF16).astype(F32)

    def weigh(r):
        for c in range(C):
            if parts == 1:
                tests = x_ref[r, c].reshape(modes, L)
            else:
                tests = jnp.concatenate(
                    [fields[1 + r][g, c].reshape(modes, L) for g in range(n_mode)], axis=0
                )
            weights[r, c * L : (c + 1) * L, :] = tests.T

    tile = 16

    def project(q, some_rows, total=None):
        for r in some_rows:
            m = [
                [jnp.broadcast_to(movers[d, r, q, j : j + 1, :], (tile, L)) for j in range(jb)]
                for d in range(2)
            ]
            rows = []
            for k in range(0, own, tile):
                parted = [[] for _ in range(jb)]
                for c in range(C):
                    lanes = slice(c * L, (c + 1) * L)
                    s0 = slopes[0, r, k : k + tile, lanes]
                    s1 = slopes[1, r, k : k + tile, lanes]
                    for j in range(jb):
                        parted[j].append((m[0][j] * s0 + m[1][j] * s1).astype(BF16))
                rows += [jnp.concatenate(parted[j], axis=1) for j in range(jb)]
            part = jnp.dot(
                jnp.concatenate(rows, axis=0), weights[r], preferred_element_type=F32
            )
            total = part if total is None else total + part
        return total

    def sort(total):
        order = [total[(k * jb + j) * tile : (k * jb + j + 1) * tile]
                 for j in range(jb) for k in range(own // tile)]
        return jnp.concatenate(order, axis=0)

    def pack(rows):
        h = rows.shape[0] // 2
        return jnp.concatenate([rows[:h], rows[h:]], axis=1)

    def to_twin(it):
        return remote(
            send1.at[it], recv1.at[it], s1_send.at[it], s1_recv.at[it], (me, twin)
        )

    def to_across(t):
        return remote(
            send2.at[t], recv2.at[t], s2_send.at[t], s2_recv.at[t], (me, across)
        )

    def to_along(t, e):
        return remote(
            send3.at[t, e], recv3.at[t, e], s3_send.at[t, e], s3_recv.at[t, e],
            (lax.rem(me + e, n_mode), along(t + 1)),
        )

    def columns(value):
        if parts == 1:
            return [value]
        low, high = pack(value[:, :modes]), pack(value[:, modes:])
        return [jnp.where(me == 0, low, high), jnp.where(me == 0, high, low)]

    def gathered(it):
        to_twin(it).wait_recv()
        return keep[it] + recv1[it].astype(F32)

    lag = min(3, nz)

    def forward_across(it):
        send2[it] = gathered(it).astype(BF16)
        to_across(it).start()

    def forward_along(it):
        t = it - nz
        value = gathered(it)
        to_across(t).wait_recv()
        for e, piece in enumerate(columns(value + recv2[t].astype(F32))):
            send3[t, e] = piece.astype(BF16)
            to_along(t, e).start()

    def step(it, carry):
        t = lax.rem(it, nz)
        column = jnp.where(it < nz, 1 - y, y)
        q = lax.rem(z + 1 + t, nz) * 2 + column
        total = sort(project(q, range(R)))
        rows = total.shape[0] // 2
        low, high = total[:rows], total[rows:]
        if parts == 1:
            low, high = pack(low), pack(high)
        keep[it] = jnp.where(core == 0, low, high)
        send1[it] = jnp.where(core == 0, high, low).astype(BF16)
        to_twin(it).start()

        @pl.when((it >= lag) & (it < lag + nz))
        def _():
            forward_across(it - lag)

        @pl.when(it >= lag + nz)
        def _():
            forward_along(it - lag)

        return carry

    for r in arrivals:
        arrive(r)
        weigh(r)
    for r in range(1, R - 1):
        prepare(r)
    arrive_halo()
    prepare(0)
    prepare(R - 1)
    lax.fori_loop(0, nq, step, 0)
    for it in range(nq - lag, nq - 1):
        forward_along(it)

    value = gathered(nq - 1)
    to_across(nz - 1).wait_recv()
    pieces = columns(value + recv2[nz - 1].astype(F32))
    if parts == 2:
        send3[nz - 1, 1] = pieces[1].astype(BF16)
        to_along(nz - 1, 1).start()
    for e in range(parts):
        value = pieces[0] if e == 0 else None
        for t in range(nz if e else nz - 1):
            to_along(t, e).wait_recv()
            got = recv3[t, e].astype(F32)
            value = got if value is None else value + got
        value = value * norm_factor
        halves = [value[:, :modes], value[:, modes:]]
        if parts == 1:
            h = value.shape[0]
            result[pl.ds(0, h), :] = halves[0]
            result[pl.ds(h, h), :] = halves[1]
        else:
            value = jnp.concatenate(halves, axis=0)
            column = me if e == 0 else 1 - me
            for j in range(value.shape[0] // own):
                start = pl.multiple_of(j * modes + column * own, own)
                result[pl.ds(start, own), :] = value[j * own : (j + 1) * own]

    out_ref[...] = result[...].T

    for d in range(1, n_mode):
        for row in range(R):
            spread(d, row).wait_send()
    for d in range(n_mode):
        @pl.when(has_left)
        def _():
            halo(d, 0).wait_send()

        @pl.when(has_right)
        def _():
            halo(d, 1).wait_send()
    for it in range(nq):
        to_twin(it).wait_send()
    for t in range(nz):
        to_across(t).wait_send()
    for t in range(nz):
        for e in range(parts):
            if t < nz - 1 or e > 0:
                to_along(t, e).wait_send()


def body(mode_fields, metric, plan):
    n_mode, n = lax.axis_size("mode"), lax.axis_size("space")
    modes, C, R, L = mode_fields.shape
    half, width = modes // 2, C * L
    norm_factor = float(R * n * L) ** (-0.5)
    out_rows = modes * modes // n
    h = out_rows // 2
    nq, nz = n // 2, n // 4
    jb = modes // nq
    parts = 2 if n_mode == 2 else 1
    dma = pltpu.SemaphoreType.DMA
    return pl.pallas_call(
        functools.partial(kernel, n_mode, n, parts, norm_factor),
        out_shape=jax.ShapeDtypeStruct((modes, out_rows), F32),
        in_specs=[
            pl.BlockSpec(memory_space=pltpu.HBM),
            pl.BlockSpec(memory_space=pltpu.HBM),
            pl.BlockSpec(memory_space=pltpu.HBM),
        ],
        out_specs=pl.BlockSpec(memory_space=pltpu.VMEM),
        scratch_shapes=[
            pltpu.VMEM(mode_fields.shape, BF16),
            pltpu.VMEM(metric.shape, F32),
            pltpu.SMEM(plan.shape[::-1], jnp.int32),
            pltpu.VMEM((out_rows, modes), F32),
            pltpu.VMEM((R, C, 2, half, L), BF16),
            pltpu.VMEM((R, width, modes * parts), BF16),
            pltpu.VMEM((2, R, modes // parts, width), F32),
            pltpu.VMEM((2, R, nq, jb, L), F32),
            pltpu.VMEM((nq, h, 2 * modes), F32),
            pltpu.VMEM((nq, h, 2 * modes), BF16),
            pltpu.VMEM((nq, h, 2 * modes), BF16),
            pltpu.VMEM((nz, h, 2 * modes), BF16),
            pltpu.VMEM((nz, h, 2 * modes), BF16),
            pltpu.VMEM((nz, parts, h // parts, 2 * modes), BF16),
            pltpu.VMEM((nz, parts, h // parts, 2 * modes), BF16),
            dma((3,)),
            dma((n_mode, R)),
            dma((n_mode, R)),
            dma((n_mode, 2)),
            dma((n_mode, 2)),
            dma((nq,)),
            dma((nq,)),
            dma((nz,)),
            dma((nz,)),
            dma((nz, parts)),
            dma((nz, parts)),
            *[pltpu.VMEM((n_mode, C, 2, half, L), BF16) for _ in range(R + 2)],
        ],
        compiler_params=pltpu.CompilerParams(
            collective_id=0, has_side_effects=True, vmem_limit_bytes=64 * 1024 * 1024 - 192 * 1024
        ),
    )(mode_fields, metric, plan.T).T


def solution(mesh):
    return jax.shard_map(
        body,
        mesh=mesh,
        in_specs=(P("mode", None, "space", None), P(None, "space", None), P()),
        out_specs=P("space", "mode"),
        check_vma=False,
    )
```

```python
import functools

import jax
import jax.numpy as jnp
from jax import lax
from jax.experimental import pallas as pl
from jax.experimental.pallas import tpu as pltpu
from jax.sharding import PartitionSpec as P

MESH = pl.DeviceIdType.MESH
F32 = jnp.float32
BF16 = jnp.bfloat16


def kernel(
    n_mode, n, parts, norm_factor,
    raw_hbm, metric_hbm, plan_hbm, out_ref,
    raw_ref, metric_ref, plan_ref, result, x_ref, weights, slopes, movers, keep, send1, recv1, send2, recv2, send3, recv3,
    load_sem, x_send, x_recv, h_send, h_recv, s1_send, s1_recv, s2_send, s2_recv, s3_send, s3_recv, *fields,
):
    R, C, _, half, L = x_ref.shape
    width = C * L
    modes = 2 * half
    own = modes // parts
    nq, nz = n // 2, n // 4
    jb = movers.shape[3]

    me = lax.axis_index("mode")
    s = lax.axis_index("space")
    core = lax.rem(s, 2)
    pair = s // 2
    y = lax.rem(pair, 2)
    z = pair // 2
    twin = s + 1 - 2 * core
    across = s + 2 - 4 * y
    has_left = s > 0
    has_right = s < n - 1
    has_other = ((core == 1) & has_right) | ((core == 0) & has_left)
    other = jnp.clip(s + 2 * core - 1, 0, n - 1)

    def along(step):
        return (lax.rem(z + step, nz) * 2 + y) * 2 + core

    load_metric = pltpu.make_async_copy(metric_hbm, metric_ref, load_sem.at[0])
    load_plan = pltpu.make_async_copy(plan_hbm, plan_ref, load_sem.at[1])
    load_raw = pltpu.make_async_copy(raw_hbm, raw_ref, load_sem.at[2])
    load_raw.start()
    load_metric.start()
    load_plan.start()

    barrier = pltpu.get_barrier_semaphore()

    def greet(device):
        pl.semaphore_signal(barrier, inc=1, device_id=device, device_id_type=MESH)

    for d in range(1, n_mode):
        greet((lax.rem(me + d, n_mode), s))
    greet((me, twin))
    greet((me, across))
    for step in range(1, nz):
        for e in range(parts):
            greet((lax.rem(me + e, n_mode), along(step)))

    @pl.when(has_other)
    def _():
        greet((me, other))

    load_raw.wait()
    for c in range(C):
        turned = jnp.swapaxes(raw_ref[:, c].astype(F32), 0, 1)
        for r in range(R):
            x_ref[r, c] = turned[r].astype(BF16).reshape(2, half, L)

    greeted = (n_mode - 1) + 2 + parts * (nz - 1)
    pl.semaphore_wait(barrier, jnp.where(has_other, greeted + 1, greeted))

    def remote(src, dst, send, recv, device):
        return pltpu.make_async_remote_copy(
            src_ref=src, dst_ref=dst, send_sem=send, recv_sem=recv,
            device_id=device, device_id_type=MESH,
        )

    def spread(d, row):
        return remote(
            x_ref.at[row], fields[1 + row].at[me],
            x_send.at[d, row], x_recv.at[d, row], (lax.rem(me + d, n_mode), s),
        )

    def halo(d, side):
        group = lax.rem(me + n_mode - d, n_mode)
        if d == 0:
            src = x_ref.at[0 if side == 0 else R - 1]
        else:
            src = fields[1 if side == 0 else R].at[group]
        target = (me, jnp.maximum(s - 1, 0)) if side == 0 else (me, jnp.minimum(s + 1, n - 1))
        return remote(
            src, fields[R + 1 if side == 0 else 0].at[group],
            h_send.at[d, side], h_recv.at[d, side], target,
        )

    arrivals = [0, R - 1] + list(range(1, R - 1))
    for row in arrivals:
        for d in range(1, n_mode):
            spread(d, row).start()

    def start_halo(d, side):
        @pl.when(has_left if side == 0 else has_right)
        def _():
            halo(d, side).start()

    start_halo(0, 0)
    start_halo(0, 1)
    for r in range(R):
        fields[1 + r][me] = x_ref[r]

    @pl.when(jnp.logical_not(has_left))
    def _():
        for g in range(n_mode):
            fields[0][g] = jnp.zeros_like(fields[0][g])

    @pl.when(jnp.logical_not(has_right))
    def _():
        for g in range(n_mode):
            fields[R + 1][g] = jnp.zeros_like(fields[R + 1][g])

    load_metric.wait()
    load_plan.wait()

    def arrive(row):
        for d in range(1, n_mode):
            spread(d, row).wait_recv()
            if row == 0:
                start_halo(d, 0)
            if row == R - 1:
                start_halo(d, 1)

    def arrive_halo():
        for d in range(n_mode):
            @pl.when(has_right)
            def _():
                halo(d, 0).wait_recv()

            @pl.when(has_left)
            def _():
                halo(d, 1).wait_recv()

    lane = lax.broadcasted_iota(jnp.int32, (half, L), 1)

    def prepare(r):
        first, second, weight = (metric_ref[i, r : r + 1, :] for i in range(3))
        for b in range(2):
            owner, which = plan_ref[0, b], plan_ref[1, b]
            for c in range(2):
                scaled = fields[1 + r][owner, c, which].astype(F32) * weight
                movers[c, r, pl.ds(b * (half // jb), half // jb)] = scaled.reshape(
                    half // jb, jb, L
                )
        for b in range(2 // parts):
            source = 2 + b if parts == 1 else 2 + me
            owner, which = plan_ref[0, source], plan_ref[1, source]
            rows = slice(b * half, (b + 1) * half)
            for c in range(C):
                lanes = slice(c * L, (c + 1) * L)
                low = fields[r][owner, c, which].astype(F32)
                mid = fields[r + 1][owner, c, which].astype(F32)
                high = fields[r + 2][owner, c, which].astype(F32)
                after = jnp.where(lane == L - 1, 0.0, pltpu.roll(mid, L - 1, 1))
                before = jnp.where(lane == 0, 0.0, pltpu.roll(mid, 1, 1))
                slopes[0, r, rows, lanes] = ((high - low) * first).astype(BF16).astype(F32)
                slopes[1, r, rows, lanes] = ((after - before) * second).astype(BF16).astype(F32)

    def weigh(r):
        for c in range(C):
            if parts == 1:
                tests = x_ref[r, c].reshape(modes, L)
            else:
                tests = jnp.concatenate(
                    [fields[1 + r][g, c].reshape(modes, L) for g in range(n_mode)], axis=0
                )
            weights[r, c * L : (c + 1) * L, :] = tests.T

    tile = 16

    def project(q, some_rows, total=None):
        for r in some_rows:
            m = [
                [jnp.broadcast_to(movers[d, r, q, j : j + 1, :], (tile, L)) for j in range(jb)]
                for d in range(2)
            ]
            rows = []
            for k in range(0, own, tile):
                parted = [[] for _ in range(jb)]
                for c in range(C):
                    lanes = slice(c * L, (c + 1) * L)
                    s0 = slopes[0, r, k : k + tile, lanes]
                    s1 = slopes[1, r, k : k + tile, lanes]
                    for j in range(jb):
                        parted[j].append((m[0][j] * s0 + m[1][j] * s1).astype(BF16))
                rows += [jnp.concatenate(parted[j], axis=1) for j in range(jb)]
            part = jnp.dot(
                jnp.concatenate(rows, axis=0), weights[r], preferred_element_type=F32
            )
            total = part if total is None else total + part
        return total

    def sort(total):
        order = [total[(k * jb + j) * tile : (k * jb + j + 1) * tile]
                 for j in range(jb) for k in range(own // tile)]
        return jnp.concatenate(order, axis=0)

    def pack(rows):
        h = rows.shape[0] // 2
        return jnp.concatenate([rows[:h], rows[h:]], axis=1)

    def to_twin(it):
        return remote(
            send1.at[it], recv1.at[it], s1_send.at[it], s1_recv.at[it], (me, twin)
        )

    def to_across(t):
        return remote(
            send2.at[t], recv2.at[t], s2_send.at[t], s2_recv.at[t], (me, across)
        )

    def to_along(t, e):
        return remote(
            send3.at[t, e], recv3.at[t, e], s3_send.at[t, e], s3_recv.at[t, e],
            (lax.rem(me + e, n_mode), along(t + 1)),
        )

    def columns(value):
        if parts == 1:
            return [value]
        low, high = pack(value[:, :modes]), pack(value[:, modes:])
        return [jnp.where(me == 0, low, high), jnp.where(me == 0, high, low)]

    def gathered(it):
        to_twin(it).wait_recv()
        return keep[it] + recv1[it].astype(F32)

    lag = min(2, nz)

    def forward_across(it):
        send2[it] = gathered(it).astype(BF16)
        to_across(it).start()

    def forward_along(it):
        t = it - nz
        value = gathered(it)
        to_across(t).wait_recv()
        for e, piece in enumerate(columns(value + recv2[t].astype(F32))):
            send3[t, e] = piece.astype(BF16)
            to_along(t, e).start()

    def step(it, carry):
        t = lax.rem(it, nz)
        column = jnp.where(it < nz, 1 - y, y)
        q = lax.rem(z + 1 + t, nz) * 2 + column
        total = sort(project(q, range(R)))
        rows = total.shape[0] // 2
        low, high = total[:rows], total[rows:]
        if parts == 1:
            low, high = pack(low), pack(high)
        keep[it] = jnp.where(core == 0, low, high)
        send1[it] = jnp.where(core == 0, high, low).astype(BF16)
        to_twin(it).start()

        @pl.when((it >= lag) & (it < lag + nz))
        def _():
            forward_across(it - lag)

        @pl.when(it >= lag + nz)
        def _():
            forward_along(it - lag)

        return carry

    for r in arrivals:
        arrive(r)
        weigh(r)
    for r in range(1, R - 1):
        prepare(r)
    arrive_halo()
    prepare(0)
    prepare(R - 1)
    lax.fori_loop(0, nq, step, 0)
    for it in range(nq - lag, nq - 1):
        forward_along(it)

    value = gathered(nq - 1)
    to_across(nz - 1).wait_recv()
    pieces = columns(value + recv2[nz - 1].astype(F32))
    if parts == 2:
        send3[nz - 1, 1] = pieces[1].astype(BF16)
        to_along(nz - 1, 1).start()
    for e in range(parts):
        value = pieces[0] if e == 0 else None
        for t in range(nz if e else nz - 1):
            to_along(t, e).wait_recv()
            got = recv3[t, e].astype(F32)
            value = got if value is None else value + got
        value = value * norm_factor
        halves = [value[:, :modes], value[:, modes:]]
        if parts == 1:
            h = value.shape[0]
            result[pl.ds(0, h), :] = halves[0]
            result[pl.ds(h, h), :] = halves[1]
        else:
            value = jnp.concatenate(halves, axis=0)
            column = me if e == 0 else 1 - me
            for j in range(value.shape[0] // own):
                start = pl.multiple_of(j * modes + column * own, own)
                result[pl.ds(start, own), :] = value[j * own : (j + 1) * own]

    out_ref[...] = result[...].T

    for d in range(1, n_mode):
        for row in range(R):
            spread(d, row).wait_send()
    for d in range(n_mode):
        @pl.when(has_left)
        def _():
            halo(d, 0).wait_send()

        @pl.when(has_right)
        def _():
            halo(d, 1).wait_send()
    for it in range(nq):
        to_twin(it).wait_send()
    for t in range(nz):
        to_across(t).wait_send()
    for t in range(nz):
        for e in range(parts):
            if t < nz - 1 or e > 0:
                to_along(t, e).wait_send()


def body(mode_fields, metric, plan):
    n_mode, n = lax.axis_size("mode"), lax.axis_size("space")
    modes, C, R, L = mode_fields.shape
    half, width = modes // 2, C * L
    norm_factor = float(R * n * L) ** (-0.5)
    out_rows = modes * modes // n
    h = out_rows // 2
    nq, nz = n // 2, n // 4
    jb = modes // nq
    parts = 2 if n_mode == 2 else 1
    dma = pltpu.SemaphoreType.DMA
    return pl.pallas_call(
        functools.partial(kernel, n_mode, n, parts, norm_factor),
        out_shape=jax.ShapeDtypeStruct((modes, out_rows), F32),
        in_specs=[
            pl.BlockSpec(memory_space=pltpu.HBM),
            pl.BlockSpec(memory_space=pltpu.HBM),
            pl.BlockSpec(memory_space=pltpu.HBM),
        ],
        out_specs=pl.BlockSpec(memory_space=pltpu.VMEM),
        scratch_shapes=[
            pltpu.VMEM(mode_fields.shape, BF16),
            pltpu.VMEM(metric.shape, F32),
            pltpu.SMEM(plan.shape[::-1], jnp.int32),
            pltpu.VMEM((out_rows, modes), F32),
            pltpu.VMEM((R, C, 2, half, L), BF16),
            pltpu.VMEM((R, width, modes * parts), BF16),
            pltpu.VMEM((2, R, modes // parts, width), F32),
            pltpu.VMEM((2, R, nq, jb, L), F32),
            pltpu.VMEM((nq, h, 2 * modes), F32),
            pltpu.VMEM((nq, h, 2 * modes), BF16),
            pltpu.VMEM((nq, h, 2 * modes), BF16),
            pltpu.VMEM((nz, h, 2 * modes), BF16),
            pltpu.VMEM((nz, h, 2 * modes), BF16),
            pltpu.VMEM((nz, parts, h // parts, 2 * modes), BF16),
            pltpu.VMEM((nz, parts, h // parts, 2 * modes), BF16),
            dma((3,)),
            dma((n_mode, R)),
            dma((n_mode, R)),
            dma((n_mode, 2)),
            dma((n_mode, 2)),
            dma((nq,)),
            dma((nq,)),
            dma((nz,)),
            dma((nz,)),
            dma((nz, parts)),
            dma((nz, parts)),
            *[pltpu.VMEM((n_mode, C, 2, half, L), BF16) for _ in range(R + 2)],
        ],
        compiler_params=pltpu.CompilerParams(
            collective_id=0, has_side_effects=True, vmem_limit_bytes=64 * 1024 * 1024 - 192 * 1024
        ),
    )(mode_fields, metric, plan.T).T


def solution(mesh):
    return jax.shard_map(
        body,
        mesh=mesh,
        in_specs=(P("mode", None, "space", None), P(None, "space", None), P()),
        out_specs=P("space", "mode"),
        check_vma=False,
    )
```
